256 devices in a mesh: row: 128 (over z, x_hi, y, core), band: 2 (over x_lo).
Axes of the slice: x: 4 (x_hi: 2, x_lo: 2; x = x_hi * 2 + x_lo), y: 4, z: 8, core: 2. Of those that a mesh axis runs over, the one named last changes fastest.
Arguments:
- intens: bfloat16 [512, 1024, 768], P('row', None, 'band'), may hold values from -6 to 6
- block_list: int32 [1024, 4], P(None, 'band'), may hold values from 0 to 2, as said below
- block_count: int32 [1024, 2], P(None, 'band'), may hold values from 0 to 2
- pixel_gradient: float32 [2, 768], P(None, 'band'), may hold values from -40 to 40
Outputs:
- image: float32 [2, 512, 1024], P('band', 'row')
The draws below stay inside these ranges and needn't reach their ends.
Inputs may be any that keep to these rules, and one draw needn't show every extreme that they name: `block_list`: the 2 entries of one scan x-frequency and band differ; entries past the count are valid block numbers and carry no weight.
All inputs are finite; a program needn't handle non-finite values.
Results may differ from the reference program's by a relative error of at most 0.0048.
Values may be sent and summed in bfloat16 or wider, within the bound.
No kernel may reach another device: no remote copies, remote signals or barrier semaphores. Data moves between devices by JAX's collectives and lax.ppermute only.
A program may use at most 128 MiB of HBM per device.

```python
import math
import jax
import jax.numpy as jnp
from jax import lax

NX = 1024
PIX_BLK = 128
BLK_BAND = 3
CAP = 2
NY = 512
PIX_BAND = 384
PIXELS = 768
N_BAND = 2


def draw_block_list(key, part):
    key = jax.random.fold_in(key, 11)
    keys = jax.random.split(key, NX * N_BAND)
    orders = jax.vmap(lambda one_key: jax.random.permutation(one_key, BLK_BAND))(keys)
    return orders[:, :CAP].reshape(NX, N_BAND * CAP).astype(jnp.int32)


def draw_block_count(key, part):
    key = jax.random.fold_in(key, 23)
    count_key, spare_key = jax.random.split(key)
    freq_index = jnp.arange(NX, dtype=jnp.int32)
    distance = jnp.minimum(freq_index, NX - freq_index)
    random_count = jax.random.randint(count_key, (NX, N_BAND), 0, CAP + 1)
    spare_mask = jax.random.randint(spare_key, (NX, N_BAND), 0, 8) == 0
    near_mask = (distance < NX // 8)[:, None]
    middle_mask = (distance < NX // 4)[:, None]
    outer_count = jnp.where(spare_mask, random_count, 0)
    return jnp.where(near_mask, CAP, jnp.where(middle_mask, random_count, outer_count)).astype(jnp.int32)


def levels(own_key, extent, pieces, least, top_value):
    def one(axis_at, shards_of):
        draws = jax.random.uniform(jax.random.fold_in(jax.random.fold_in(own_key, 6), axis_at), (shards_of,), jnp.float32, least / len(pieces), top_value / len(pieces))
        return jnp.repeat(jnp.exp(draws), extent[axis_at] // shards_of).reshape((-1,) + (1,) * (len(extent) - axis_at - 1))

    loudness = one(*pieces[0])
    for cut in pieces[1:]:
        loudness = loudness * one(*cut)
    return loudness


def scatter_about(own_key, dims, deviation, limit, shards=(), kind=jnp.bfloat16):
    values = deviation * jax.random.normal(own_key, dims, jnp.float32)
    if shards:
        values = values * levels(own_key, dims, shards, -0.22, 0.18)
    return jnp.clip(values, -limit, limit).astype(kind)


def setup_inputs(seed: int = 0) -> dict:
    key_list = jax.random.split(jax.random.key(seed), 5)
    return {
        "intens": scatter_about(key_list[0], (NY, NX, PIXELS), 1.0, 6.0, ((0, 128), (2, 2))),
        "block_list": draw_block_list(jax.random.fold_in(key_list[4], 71), 0),
        "block_count": draw_block_count(jax.random.fold_in(key_list[4], 71), 0),
        "pixel_gradient": jnp.clip(jax.random.uniform(key_list[3], (2, PIXELS), jnp.float32, -40.0, 40.0) * levels(key_list[3], (2, PIXELS), ((1, 2),), -0.4, 0.0), -40.0, 40.0),
    }


def factor_pair(rows_index, cols_index, length):
    turns = rows_index[:, None] * cols_index[None, :] % length
    angle = turns.astype(jnp.float32) * (2.0 * math.pi / length)
    norm_factor = 1.0 / math.sqrt(length)
    return (jnp.cos(angle) * norm_factor, jnp.sin(angle) * norm_factor)

def signed_freq(index_values, length):
    return jnp.where(index_values < length // 2, index_values, index_values - length).astype(jnp.float32) / length

def rounded(values):
    return lax.optimization_barrier(values.astype(jnp.bfloat16)).astype(jnp.float32)

def rotation_table(cosine_part, sine_part):
    upper_half = jnp.concatenate([cosine_part, sine_part], axis=1)
    lower_half = jnp.concatenate([-sine_part, cosine_part], axis=1)
    return jnp.concatenate([upper_half, lower_half], axis=0)

def reference(intens, block_list, block_count, pixel_gradient):
    every_x = jnp.arange(NX, dtype=jnp.int32)
    every_y = jnp.arange(NY, dtype=jnp.int32)
    cosine_x, sine_x = factor_pair(every_x, every_x, NX)
    table_x = rounded(jnp.concatenate([cosine_x, -sine_x], axis=0))
    cosine_y, sine_y = factor_pair(every_y, every_y, NY)
    exact_y = rotation_table(cosine_y, sine_y)
    forward_y = rounded(exact_y)
    pixel_total = N_BAND * PIX_BAND
    flat_intens = jnp.transpose(intens, (1, 0, 2)).reshape(NX, NY * pixel_total).astype(jnp.float32)
    freq_x = signed_freq(every_x, NX)
    freq_y = signed_freq(every_y, NY)
    gradient = pixel_gradient.reshape(2, N_BAND, BLK_BAND, PIX_BLK)
    band_rows = jnp.arange(N_BAND, dtype=jnp.int32)[:, None]
    slot_index = jnp.arange(CAP, dtype=jnp.int32)
    psi_scale = 1.0 / math.sqrt(N_BAND * CAP * PIX_BLK)
    group_size = math.gcd(NX, 32)
    slot_width = N_BAND * CAP * PIX_BLK

    def one_group(start_index):
        table_rows = jnp.concatenate([lax.dynamic_slice_in_dim(table_x, start_index, group_size, 0), lax.dynamic_slice_in_dim(table_x, NX + start_index, group_size, 0)], axis=0)
        spectrum = jnp.dot(table_rows, flat_intens, preferred_element_type=jnp.float32)
        spectrum = rounded(spectrum).reshape(2, group_size, NY, N_BAND, BLK_BAND, PIX_BLK)

        def one_freq(offset):
            freq_index = start_index + offset
            block_ids = lax.dynamic_index_in_dim(block_list, freq_index, 0, keepdims=False).reshape(N_BAND, CAP)
            counts = lax.dynamic_index_in_dim(block_count, freq_index, 0, keepdims=False)
            local_spec = lax.dynamic_index_in_dim(spectrum, offset, 1, keepdims=False)
            picked = local_spec[:, :, band_rows, block_ids]
            along_y = jnp.dot(forward_y, picked.reshape(2 * NY, slot_width), preferred_element_type=jnp.float32)
            real_part = along_y[:NY]
            imag_part = along_y[NY:]
            gradient_x = gradient[0][band_rows, block_ids].reshape(slot_width)
            gradient_y = gradient[1][band_rows, block_ids].reshape(slot_width)
            live_mask = (slot_index[None, :] < counts[:, None]).astype(jnp.float32)
            weight = jnp.broadcast_to(live_mask[:, :, None], (N_BAND, CAP, PIX_BLK)).reshape(slot_width)
            freq_now = lax.dynamic_index_in_dim(freq_x, freq_index, 0, keepdims=False)
            phase_angle = (gradient_x[None, :] * freq_now + gradient_y[None, :] * freq_y[:, None]) * (2.0 * math.pi)
            cosine_t = jnp.cos(phase_angle)
            sine_t = jnp.sin(phase_angle)
            psi_real = lax.optimization_barrier(jnp.sum((real_part * cosine_t + imag_part * sine_t) * weight[None, :], axis=1))
            psi_imag = lax.optimization_barrier(jnp.sum((imag_part * cosine_t - real_part * sine_t) * weight[None, :], axis=1))
            return jnp.stack([psi_real, psi_imag]) * psi_scale
        return lax.map(one_freq, jnp.arange(group_size, dtype=jnp.int32))
    starts = jnp.arange(NX // group_size, dtype=jnp.int32) * group_size
    psi = lax.map(one_group, starts).reshape(NX, 2 * NY)
    columns = jnp.dot(psi, exact_y, precision=lax.Precision.HIGHEST, preferred_element_type=jnp.float32)
    column_real = columns[:, :NY].T
    column_imag = columns[:, NY:].T
    back_x = rotation_table(cosine_x, sine_x)
    image = jnp.dot(jnp.concatenate([column_real, column_imag], axis=1), back_x, precision=lax.Precision.HIGHEST, preferred_element_type=jnp.float32)
    return jnp.stack([image[:, :NX], image[:, NX:]])
```

```python
import math

import jax
import jax.numpy as jnp
import ml_dtypes
import numpy as np
from jax import lax
from jax.experimental import pallas as pl
from jax.experimental.pallas import tpu as pltpu
from jax.sharding import Mesh
from jax.sharding import PartitionSpec as P

NX = 1024
NY = 512
PIX_BLK = 128
BLK_BAND = 3
PIX_BAND = PIX_BLK * BLK_BAND
ROWS_DEV = 4
CAP = 2
HALF_X = NX // 2
CHUNK = 256
STEPS = HALF_X // CHUNK
GROUP = ROWS_DEV * PIX_BLK
DEPTH = BLK_BAND * GROUP
TALL = NY + 16
GRID_Z, GRID_XH, GRID_Y, GRID_CORE, GRID_BAND = 8, 2, 4, 2, 2
ROW_AXES = ("z", "xh", "y", "core")
F32, BF16 = jnp.float32, jnp.bfloat16


def forward_table():
    turns = np.outer(np.arange(HALF_X + 1), np.arange(NX)) % NX
    angle = turns.astype(np.float32) * np.float32(2.0 * math.pi / NX)
    norm_factor = np.float32(1.0 / math.sqrt(NX))
    cosine, sine = np.cos(angle) * norm_factor, np.sin(angle) * norm_factor
    lower = -sine[:HALF_X]
    lower[0] = cosine[HALF_X]
    pieces = np.stack(
        [cosine[:HALF_X].reshape(STEPS, CHUNK, NX), lower.reshape(STEPS, CHUNK, NX)], axis=1
    )
    return pieces.reshape(NX, NX).astype(ml_dtypes.bfloat16)


def backward_table():
    turns = np.outer(np.arange(HALF_X + 1), np.arange(NX)) % NX
    angle = turns.astype(np.float64) * (2.0 * math.pi / NX)
    scale = 1.0 / math.sqrt(NX) / math.sqrt(GRID_BAND * CAP * PIX_BLK)
    upper = np.cos(angle[:HALF_X]) * scale
    upper[0] *= 0.5
    lower = -np.sin(angle[:HALF_X]) * scale
    lower[0] = np.cos(angle[HALF_X]) * scale
    pieces = np.stack(
        [upper.reshape(STEPS, CHUNK, NX), lower.reshape(STEPS, CHUNK, NX)], axis=1
    )
    whole = pieces.reshape(NX, NX).astype(np.float32)
    high = whole.astype(ml_dtypes.bfloat16)
    low = (whole - high.astype(np.float32)).astype(ml_dtypes.bfloat16)
    return high, low


def horner(variable, coefficients):
    total = jnp.full_like(variable, coefficients[-1])
    for coefficient in coefficients[-2::-1]:
        total = total * variable + coefficient
    return total


SINE = [(-1.0) ** k / math.factorial(2 * k + 1) for k in range(8)]
COSINE = [(-1.0) ** k / math.factorial(2 * k) for k in range(8)]


def small_sincos(angle):
    square = angle * angle
    return angle * horner(square, SINE), horner(square, COSINE)


def cycles_sincos(cycles):
    cycles = cycles - jnp.round(cycles)
    sine, cosine = small_sincos(cycles * math.pi)
    return 2.0 * sine * cosine, 1.0 - 2.0 * sine * sine


def local_kernel(
    place_ref,
    masks_ref,
    gradient_ref,
    table_ref,
    intens_ref,
    keep_ref,
    send_ref,
    values,
    shift_base,
    shift_table,
    coarse,
    fine,
    phase,
    rotated,
    lone,
    products,
    lone_out,
    copy_sem,
):
    step = pl.program_id(0)
    own_row = place_ref[0]
    own_core = place_ref[1]

    def copies():
        for block in range(BLK_BAND):
            for row in range(ROWS_DEV):
                yield pltpu.make_async_copy(
                    intens_ref.at[row, :, pl.ds(block * PIX_BLK, PIX_BLK)],
                    values.at[:, pl.ds(block * GROUP + row * PIX_BLK, PIX_BLK)],
                    copy_sem.at[block * ROWS_DEV + row],
                )

    @pl.when(step == 0)
    def prepare():
        for copy in copies():
            copy.start()
        gradient_x = gradient_ref[0:1, :]
        gradient_y = gradient_ref[1:2, :]
        nearest = jnp.round(gradient_y)
        rest = gradient_y - nearest
        sinc = horner(
            rest * rest, [SINE[k] * math.pi ** (2 * k) for k in range(8)]
        )
        small = rest * (math.pi / NY)
        peak = sinc * (1.0 - small * small * (1.0 / 3.0))
        parity = nearest - 2.0 * jnp.floor(nearest * 0.5)
        lobes = (1.0 - 2.0 * parity) * (rest * math.pi) * sinc * (1.0 / NY)
        sine_g, cosine_g = small_sincos(gradient_y * (math.pi / NY))
        index = lax.broadcasted_iota(jnp.int32, (TALL, PIX_BLK), 0)
        offset = index - (ROWS_DEV - 1) - ROWS_DEV * own_row
        distance = offset.astype(F32)
        folded = distance - NY * jnp.round(distance * (1.0 / NY))
        sine_d, cosine_d = small_sincos(folded * (math.pi / NY))
        row_sign = (1 - 2 * (offset & 1)).astype(F32)
        for block in range(BLK_BAND):
            lanes = slice(block * PIX_BLK, (block + 1) * PIX_BLK)
            upper = (cosine_d * cosine_g[:, lanes] + sine_d * sine_g[:, lanes]) * row_sign
            lower = sine_d * cosine_g[:, lanes] - cosine_d * sine_g[:, lanes]
            turns = (distance - nearest[:, lanes]) * (1.0 / NY)
            at_peak = turns == jnp.round(turns)
            lower = jnp.where(at_peak, 1.0, lower)
            shift_base[:, lanes] = jnp.where(
                at_peak, peak[:, lanes], -lobes[:, lanes] * upper / lower
            )
        first_row = lax.broadcasted_iota(jnp.int32, (TALL - NY, PIX_BLK), 0) == 0
        for block in range(BLK_BAND):
            lanes = slice(block * PIX_BLK, (block + 1) * PIX_BLK)
            for row in range(ROWS_DEV):
                column = block * GROUP + row * PIX_BLK
                start = ROWS_DEV - 1 - row
                shift_table[0:NY, column : column + PIX_BLK] = shift_base[
                    start : start + NY, lanes
                ].astype(BF16)
                shift_table[NY:TALL, column : column + PIX_BLK] = jnp.where(
                    first_row, lobes[:, lanes] * (1.0 - 2.0 * (row % 2)), 0.0
                ).astype(BF16)
        eights = lax.broadcasted_iota(jnp.int32, (HALF_X // 8, PIX_BAND), 0).astype(F32)
        coarse[0], coarse[1] = cycles_sincos(gradient_x * (eights * (8.0 / NX)))
        units = lax.broadcasted_iota(jnp.int32, (8, PIX_BAND), 0).astype(F32)
        fine[0], fine[1] = cycles_sincos(gradient_x * (units * (1.0 / NX)))
        lone[...] = jnp.zeros_like(lone)
        for copy in copies():
            copy.wait()

    for octet in range(CHUNK // 8):
        at_octet = pl.ds(step * (CHUNK // 8) + octet, 1)
        sine_c, cosine_c = coarse[0, at_octet, :], coarse[1, at_octet, :]
        rows = slice(octet * 8, octet * 8 + 8)
        phase[0, rows, :] = sine_c * fine[1] + cosine_c * fine[0]
        phase[1, rows, :] = cosine_c * fine[1] - sine_c * fine[0]

    contract_last = (((1,), (1,)), ((), ()))
    for block in range(BLK_BAND):
        columns = slice(block * GROUP, (block + 1) * GROUP)
        lanes = slice(block * PIX_BLK, (block + 1) * PIX_BLK)
        spectrum = jnp.dot(table_ref[...], values[:, columns], preferred_element_type=F32)
        spectrum = spectrum.astype(BF16).astype(F32)
        sine_p, cosine_p = phase[0, :, lanes], phase[1, :, lanes]
        for row in range(ROWS_DEV):
            inner = slice(row * PIX_BLK, (row + 1) * PIX_BLK)
            outer = slice(block * GROUP + row * PIX_BLK, block * GROUP + (row + 1) * PIX_BLK)
            real_part = spectrum[:CHUNK, inner]
            imag_part = spectrum[CHUNK:, inner]
            rotated[:CHUNK, outer] = (real_part * cosine_p + imag_part * sine_p).astype(BF16)
            rotated[CHUNK:, outer] = (imag_part * cosine_p - real_part * sine_p).astype(BF16)

        @pl.when(step == 0)
        def middle():
            sine_m, cosine_m = cycles_sincos(gradient_ref[0:1, lanes] * 0.5)
            weight = masks_ref[2 * BLK_BAND + block : 2 * BLK_BAND + block + 1, 0:PIX_BLK]
            top = lax.broadcasted_iota(jnp.int32, (16, PIX_BLK), 0) == 0
            for row in range(ROWS_DEV):
                inner = slice(row * PIX_BLK, (row + 1) * PIX_BLK)
                outer = slice(block * GROUP + row * PIX_BLK, block * GROUP + (row + 1) * PIX_BLK)
                only = spectrum[CHUNK : CHUNK + 1, inner] * weight
                lone[0:16, outer] = jnp.where(top, only * cosine_m, 0.0).astype(BF16)
                lone[PIX_BLK : PIX_BLK + 16, outer] = jnp.where(
                    top, only * sine_m, 0.0
                ).astype(BF16)

        products[block] = lax.dot_general(
            shift_table[:, columns],
            rotated[:, columns],
            contract_last,
            preferred_element_type=F32,
        )

    @pl.when(step == 0)
    def middle_out():
        both = lax.dot_general(
            shift_table[...], lone[...], contract_last, preferred_element_type=F32
        )
        even = (lax.broadcasted_iota(jnp.int32, (NY, PIX_BLK), 0) & 1) == 0
        one = both[NY : NY + 1, PIX_BLK:]
        lone_out[0] = both[:NY, :PIX_BLK] - jnp.where(even, one, -one)
        one = both[NY : NY + 1, :PIX_BLK]
        lone_out[1] = both[:NY, PIX_BLK:] + jnp.where(even, one, -one)

    sums = masks_ref[0:BLK_BAND, pl.ds(step * CHUNK, CHUNK)]
    differences = masks_ref[BLK_BAND : 2 * BLK_BAND, pl.ds(step * CHUNK, CHUNK)]
    edge = jnp.zeros((4, CHUNK), F32)
    sum_edge_real = sum_edge_imag = diff_edge_real = diff_edge_imag = edge[0:1]
    for block in range(BLK_BAND):
        edge_real = products[block, NY : NY + 1, :CHUNK]
        edge_imag = products[block, NY : NY + 1, CHUNK:]
        sum_edge_real = sum_edge_real + differences[block : block + 1] * edge_real
        sum_edge_imag = sum_edge_imag + differences[block : block + 1] * edge_imag
        diff_edge_real = diff_edge_real + sums[block : block + 1] * edge_real
        diff_edge_imag = diff_edge_imag + sums[block : block + 1] * edge_imag
    even = (lax.broadcasted_iota(jnp.int32, (8, CHUNK), 0) & 1) == 0
    alternating = jnp.where(even, 1.0, -1.0)
    add_hr = -alternating * sum_edge_imag
    add_hi = alternating * sum_edge_real
    add_gr = -alternating * diff_edge_imag
    add_gi = alternating * diff_edge_real
    lane_zero = (lax.broadcasted_iota(jnp.int32, (8, PIX_BLK), 1) == 0) & (step == 0)

    def tile(start):
        rows = slice(start, start + 8)
        herm_real, herm_imag, anti_real, anti_imag = add_hr, add_hi, add_gr, add_gi
        for block in range(BLK_BAND):
            real_part = products[block, rows, :CHUNK]
            imag_part = products[block, rows, CHUNK:]
            herm_real = herm_real + sums[block : block + 1] * real_part
            herm_imag = herm_imag + sums[block : block + 1] * imag_part
            anti_real = anti_real + differences[block : block + 1] * real_part
            anti_imag = anti_imag + differences[block : block + 1] * imag_part

        def mend(part, which):
            first = jnp.where(lane_zero, lone_out[which, rows, :], part[:, :PIX_BLK])
            return jnp.concatenate([first, part[:, PIX_BLK:]], axis=1)

        return (
            (herm_real, mend(herm_imag, 0)),
            (anti_imag, mend(-anti_real, 1)),
        )

    upper_rows = lax.broadcasted_iota(jnp.int32, (8, CHUNK), 0) < ROWS_DEV
    first_core = jnp.full((8, CHUNK), own_core, jnp.int32) == 0

    def split_pair(left, right):
        low = jnp.where(upper_rows, left, pltpu.roll(right, ROWS_DEV, 0))
        high = jnp.where(upper_rows, pltpu.roll(left, ROWS_DEV, 0), right)
        return jnp.where(first_core, low, high), jnp.where(first_core, high, low)

    for x_high in range(GRID_XH):
        for y_at in range(GRID_Y):
            for quad in range(GRID_Z // 4):
                pairs = []
                for pair in range(2):
                    z_at = quad * 4 + pair * 2
                    start = z_at * 64 + x_high * 32 + y_at * 8
                    pairs.append((tile(start), tile(start + 64)))
                target = x_high * 128 + y_at * 32 + quad * 16
                rows = slice(target, target + 16)
                for band in range(GRID_BAND):
                    for part in range(2):
                        lanes = slice(part * CHUNK, (part + 1) * CHUNK)
                        kept, sent = [], []
                        for left, right in pairs:
                            own, other = split_pair(left[band][part], right[band][part])
                            kept.append(own)
                            sent.append(other)
                        keep_ref[band, rows, lanes] = jnp.concatenate(kept, axis=0).astype(BF16)
                        send_ref[band, rows, lanes] = jnp.concatenate(sent, axis=0).astype(BF16)


def local_part(place, masks, gradient, table, intens):
    out_block = pl.BlockSpec((GRID_BAND, NY // 2, 2 * CHUNK), lambda i: (0, 0, i))
    out_shape = jax.ShapeDtypeStruct((GRID_BAND, NY // 2, NX), BF16)
    return pl.pallas_call(
        local_kernel,
        grid=(STEPS,),
        in_specs=[
            pl.BlockSpec(memory_space=pltpu.SMEM),
            pl.BlockSpec((16, HALF_X), lambda i: (0, 0)),
            pl.BlockSpec((2, PIX_BAND), lambda i: (0, 0)),
            pl.BlockSpec((2 * CHUNK, NX), lambda i: (i, 0)),
            pl.BlockSpec(memory_space=pl.ANY),
        ],
        out_specs=[out_block, out_block],
        out_shape=[out_shape, out_shape],
        scratch_shapes=[
            pltpu.VMEM((NX, DEPTH), BF16),
            pltpu.VMEM((TALL, PIX_BAND), F32),
            pltpu.VMEM((TALL, DEPTH), BF16),
            pltpu.VMEM((2, HALF_X // 8, PIX_BAND), F32),
            pltpu.VMEM((2, 8, PIX_BAND), F32),
            pltpu.VMEM((2, CHUNK, PIX_BAND), F32),
            pltpu.VMEM((2 * CHUNK, DEPTH), BF16),
            pltpu.VMEM((2 * PIX_BLK, DEPTH), BF16),
            pltpu.VMEM((BLK_BAND, TALL, 2 * CHUNK), F32),
            pltpu.VMEM((2, NY, PIX_BLK), F32),
            pltpu.SemaphoreType.DMA((BLK_BAND * ROWS_DEV,)),
        ],
        compiler_params=pltpu.CompilerParams(vmem_limit_bytes=48 * 1024 * 1024),
    )(place, masks, gradient, table, intens)


def final_kernel(parts_ref, high_ref, low_ref, image_ref):
    total = parts_ref[0].astype(F32)
    for source in range(1, GRID_Z):
        total = total + parts_ref[source].astype(F32)
    high = total.astype(BF16)
    low = (total - high.astype(F32)).astype(BF16)
    image = jnp.dot(high, high_ref[...], preferred_element_type=F32)
    image = image + jnp.dot(low, high_ref[...], preferred_element_type=F32)
    image_ref[0] = image + jnp.dot(high, low_ref[...], preferred_element_type=F32)


def final_part(parts, high, low):
    return pl.pallas_call(
        final_kernel,
        out_shape=jax.ShapeDtypeStruct((1, ROWS_DEV, NX), F32),
        compiler_params=pltpu.CompilerParams(vmem_limit_bytes=32 * 1024 * 1024),
    )(parts, high, low)


def used_masks(block_list, block_count):
    block_ids = jnp.arange(BLK_BAND, dtype=jnp.int32)[:, None, None]
    live = jnp.arange(CAP, dtype=jnp.int32)[None, :] < block_count
    used = jnp.any((block_list[None] == block_ids) & live[None], axis=-1).astype(F32)
    mirror = jnp.concatenate([used[:, :1], used[:, :HALF_X:-1]], axis=1)
    ahead = used[:, :HALF_X]
    middle = jnp.broadcast_to(used[:, HALF_X : HALF_X + 1], (BLK_BAND, HALF_X))
    spare = jnp.zeros((16 - 3 * BLK_BAND, HALF_X), F32)
    return jnp.concatenate([ahead + mirror, ahead - mirror, middle, spare], axis=0)


def body(intens, block_list, block_count, pixel_gradient):
    own_row = lax.axis_index(ROW_AXES)
    own_core = lax.axis_index("core")
    place = jnp.stack([own_row, own_core]).astype(jnp.int32)
    masks = used_masks(block_list, block_count)
    keep, send = local_part(
        place, masks, pixel_gradient, jnp.asarray(forward_table()), intens
    )
    received = lax.ppermute(send, "core", [(0, 1), (1, 0)])
    chip = (keep.astype(F32) + received.astype(F32)).astype(BF16)
    chip = chip.reshape(GRID_BAND * GRID_XH * GRID_Y, 4 * GRID_Z, NX)
    spread = lax.all_to_all(
        chip, ("band", "xh", "y"), split_axis=0, concat_axis=0, tiled=True
    )
    plane = jnp.sum(spread.astype(F32), axis=0).astype(BF16)
    plane = plane.reshape(GRID_Z, ROWS_DEV, NX)
    parts = lax.all_to_all(plane, "z", split_axis=0, concat_axis=0, tiled=True)
    high, low = backward_table()
    return final_part(parts, jnp.asarray(high), jnp.asarray(low))


def solution(mesh):
    grid = Mesh(
        mesh.devices.reshape(GRID_Z, GRID_XH, GRID_Y, GRID_CORE, GRID_BAND),
        ROW_AXES + ("band",),
    )
    return jax.shard_map(
        body,
        mesh=grid,
        in_specs=(P(ROW_AXES, None, "band"), P(None, "band"), P(None, "band"), P(None, "band")),
        out_specs=P("band", ROW_AXES, None),
        check_vma=False,
    )
```

```python
import math

import jax
import jax.numpy as jnp
import ml_dtypes
import numpy as np
from jax import lax
from jax.experimental import pallas as pl
from jax.experimental.pallas import tpu as pltpu
from jax.sharding import Mesh
from jax.sharding import PartitionSpec as P

NX = 1024
NY = 512
PIX_BLK = 128
BLK_BAND = 3
PIX_BAND = PIX_BLK * BLK_BAND
ROWS_DEV = 4
CAP = 2
HALF_X = NX // 2
CHUNK = 256
STEPS = HALF_X // CHUNK
GROUP = ROWS_DEV * PIX_BLK
DEPTH = BLK_BAND * GROUP
TALL = NY + 16
GRID_Z, GRID_XH, GRID_Y, GRID_CORE, GRID_BAND = 8, 2, 4, 2, 2
PIECES = GRID_XH * GRID_Y * GRID_BAND
ROW_AXES = ("z", "xh", "y", "core")
F32, BF16 = jnp.float32, jnp.bfloat16


def forward_table():
    turns = np.outer(np.arange(HALF_X + 1), np.arange(NX)) % NX
    angle = turns.astype(np.float32) * np.float32(2.0 * math.pi / NX)
    norm_factor = np.float32(1.0 / math.sqrt(NX))
    cosine, sine = np.cos(angle) * norm_factor, np.sin(angle) * norm_factor
    lower = -sine[:HALF_X]
    lower[0] = cosine[HALF_X]
    pieces = np.stack(
        [cosine[:HALF_X].reshape(STEPS, CHUNK, NX), lower.reshape(STEPS, CHUNK, NX)], axis=1
    )
    return pieces.reshape(NX, NX).astype(ml_dtypes.bfloat16)


def backward_table():
    turns = np.outer(np.arange(HALF_X + 1), np.arange(NX)) % NX
    angle = turns.astype(np.float64) * (2.0 * math.pi / NX)
    scale = 1.0 / math.sqrt(NX) / math.sqrt(GRID_BAND * CAP * PIX_BLK)
    upper = np.cos(angle[:HALF_X]) * scale
    upper[0] *= 0.5
    lower = -np.sin(angle[:HALF_X]) * scale
    lower[0] = np.cos(angle[HALF_X]) * scale
    pieces = np.stack(
        [upper.reshape(STEPS, CHUNK, NX), lower.reshape(STEPS, CHUNK, NX)], axis=1
    )
    whole = pieces.reshape(NX, NX).astype(np.float32)
    high = whole.astype(ml_dtypes.bfloat16)
    low = (whole - high.astype(np.float32)).astype(ml_dtypes.bfloat16)
    return np.stack([high, low])


def horner(variable, coefficients):
    total = jnp.full_like(variable, coefficients[-1])
    for coefficient in coefficients[-2::-1]:
        total = total * variable + coefficient
    return total


SINE = [(-1.0) ** k / math.factorial(2 * k + 1) for k in range(8)]
COSINE = [(-1.0) ** k / math.factorial(2 * k) for k in range(8)]


def small_sincos(angle):
    square = angle * angle
    return angle * horner(square, SINE), horner(square, COSINE)


def cycles_sincos(cycles):
    cycles = cycles - jnp.round(cycles)
    sine, cosine = small_sincos(cycles * math.pi)
    return 2.0 * sine * cosine, 1.0 - 2.0 * sine * sine


def own_place():
    z_at, x_high, y_at, core = (lax.axis_index(name) for name in ROW_AXES)
    return ((z_at * GRID_XH + x_high) * GRID_Y + y_at) * GRID_CORE + core, core


def local_kernel(
    lists_hbm,
    counts_hbm,
    gradient_hbm,
    table_hbm,
    intens_hbm,
    keep_ref,
    send_ref,
    lists_ref,
    counts_ref,
    gradient_ref,
    table_ref,
    values,
    shift_base,
    shift_table,
    rotated,
    lone,
    products,
    lone_out,
    copy_sem,
):
    own_row, own_core = own_place()
    small_copies = [
        pltpu.make_async_copy(gradient_hbm, gradient_ref, copy_sem.at[0]),
        pltpu.make_async_copy(lists_hbm, lists_ref, copy_sem.at[1]),
        pltpu.make_async_copy(counts_hbm, counts_ref, copy_sem.at[2]),
    ]
    table_copies = []
    for step in range(STEPS):
        rows = pl.ds(step * 2 * CHUNK, 2 * CHUNK)
        table_copies.append(
            pltpu.make_async_copy(table_hbm.at[rows], table_ref.at[rows], copy_sem.at[3 + step])
        )
    block_copies = []
    for block in range(BLK_BAND):
        block_copies.append([])
        for row in range(ROWS_DEV):
            block_copies[block].append(
                pltpu.make_async_copy(
                    intens_hbm.at[row, :, pl.ds(block * PIX_BLK, PIX_BLK)],
                    values.at[:, pl.ds(block * GROUP + row * PIX_BLK, PIX_BLK)],
                    copy_sem.at[3 + STEPS + block * ROWS_DEV + row],
                )
            )
    for copy in small_copies:
        copy.start()
    table_copies[0].start()
    for copy in sum(block_copies, []):
        copy.start()
    for copy in table_copies[1:]:
        copy.start()
    for copy in small_copies:
        copy.wait()

    gradient_x = gradient_ref[0:1, :]
    gradient_y = gradient_ref[1:2, :]
    nearest = jnp.round(gradient_y)
    rest = gradient_y - nearest
    sinc = horner(rest * rest, [SINE[k] * math.pi ** (2 * k) for k in range(8)])
    small = rest * (math.pi / NY)
    peak = sinc * (1.0 - small * small * (1.0 / 3.0))
    parity = nearest - 2.0 * jnp.floor(nearest * 0.5)
    lobes = (1.0 - 2.0 * parity) * (rest * math.pi) * sinc * (1.0 / NY)
    sine_g, cosine_g = small_sincos(gradient_y * (math.pi / NY))
    index = lax.broadcasted_iota(jnp.int32, (TALL, PIX_BLK), 0)
    offset = index - (ROWS_DEV - 1) - ROWS_DEV * own_row
    distance = offset.astype(F32)
    folded = distance - NY * jnp.round(distance * (1.0 / NY))
    sine_d, cosine_d = small_sincos(folded * (math.pi / NY))
    row_sign = (1 - 2 * (offset & 1)).astype(F32)
    first_row = lax.broadcasted_iota(jnp.int32, (TALL - NY, PIX_BLK), 0) == 0
    for block in range(BLK_BAND):
        lanes = slice(block * PIX_BLK, (block + 1) * PIX_BLK)
        upper = (cosine_d * cosine_g[:, lanes] + sine_d * sine_g[:, lanes]) * row_sign
        lower = sine_d * cosine_g[:, lanes] - cosine_d * sine_g[:, lanes]
        turns = (distance - nearest[:, lanes]) * (1.0 / NY)
        at_peak = turns == jnp.round(turns)
        lower = jnp.where(at_peak, 1.0, lower)
        shift_base[:, lanes] = jnp.where(
            at_peak, peak[:, lanes], -lobes[:, lanes] * upper / lower
        )
        for row in range(ROWS_DEV):
            column = block * GROUP + row * PIX_BLK
            start = ROWS_DEV - 1 - row
            shift_table[0:NY, column : column + PIX_BLK] = shift_base[
                start : start + NY, lanes
            ].astype(BF16)
            shift_table[NY:TALL, column : column + PIX_BLK] = jnp.where(
                first_row, lobes[:, lanes] * (1.0 - 2.0 * (row % 2)), 0.0
            ).astype(BF16)

    eights = lax.broadcasted_iota(jnp.int32, (HALF_X // 8, PIX_BAND), 0).astype(F32)
    coarse_sine, coarse_cosine = cycles_sincos(gradient_x * (eights * (8.0 / NX)))
    units = lax.broadcasted_iota(jnp.int32, (8, PIX_BAND), 0).astype(F32)
    fine_sine, fine_cosine = cycles_sincos(gradient_x * (units * (1.0 / NX)))
    middle_sine, middle_cosine = cycles_sincos(gradient_x * 0.5)

    block_ids = lax.broadcasted_iota(jnp.int32, (8, NX), 0)
    counts = counts_ref[0:1, :]
    used = ((lists_ref[0:1, :] == block_ids) & (counts > 0)) | (
        (lists_ref[1:2, :] == block_ids) & (counts > 1)
    )
    used = used.astype(F32)
    place_sum = lax.broadcasted_iota(jnp.int32, (HALF_X, HALF_X), 0) + lax.broadcasted_iota(
        jnp.int32, (HALF_X, HALF_X), 1
    )
    reverse = (place_sum == HALF_X).astype(F32).astype(BF16)
    mirror = jnp.dot(used[:, HALF_X:].astype(BF16), reverse, preferred_element_type=F32)
    lane_first = lax.broadcasted_iota(jnp.int32, (8, HALF_X), 1) == 0
    ahead = used[:, :HALF_X]
    mirror = jnp.where(lane_first, ahead, mirror)
    every_sum = ahead + mirror
    every_difference = ahead - mirror

    contract_last = (((1,), (1,)), ((), ()))
    even = (lax.broadcasted_iota(jnp.int32, (8, CHUNK), 0) & 1) == 0
    alternating = jnp.where(even, 1.0, -1.0)
    upper_rows = lax.broadcasted_iota(jnp.int32, (8, PIX_BLK), 0) < ROWS_DEV
    first_core = jnp.full((8, PIX_BLK), own_core, jnp.int32) == 0
    lane_zero = lax.broadcasted_iota(jnp.int32, (8, PIX_BLK), 1) == 0
    lone[...] = jnp.zeros_like(lone)

    for step in range(STEPS):
        table_copies[step].wait()
        table = table_ref[step * 2 * CHUNK : (step + 1) * 2 * CHUNK, :]
        for block in range(BLK_BAND):
            columns = slice(block * GROUP, (block + 1) * GROUP)
            lanes = slice(block * PIX_BLK, (block + 1) * PIX_BLK)
            if step == 0:
                for copy in block_copies[block]:
                    copy.wait()
            spectrum = jnp.dot(table, values[:, columns], preferred_element_type=F32)
            spectrum = spectrum.astype(BF16).astype(F32)
            sines, cosines = [], []
            for octet in range(step * CHUNK // 8, (step + 1) * CHUNK // 8):
                sine_c = coarse_sine[octet : octet + 1, lanes]
                cosine_c = coarse_cosine[octet : octet + 1, lanes]
                sines.append(sine_c * fine_cosine[:, lanes] + cosine_c * fine_sine[:, lanes])
                cosines.append(cosine_c * fine_cosine[:, lanes] - sine_c * fine_sine[:, lanes])
            sine_p = jnp.concatenate(sines, axis=0)
            cosine_p = jnp.concatenate(cosines, axis=0)
            for row in range(ROWS_DEV):
                inner = slice(row * PIX_BLK, (row + 1) * PIX_BLK)
                outer = slice(
                    block * GROUP + row * PIX_BLK, block * GROUP + (row + 1) * PIX_BLK
                )
                real_part = spectrum[:CHUNK, inner]
                imag_part = spectrum[CHUNK:, inner]
                rotated[:CHUNK, outer] = (
                    real_part * cosine_p + imag_part * sine_p
                ).astype(BF16)
                rotated[CHUNK:, outer] = (
                    imag_part * cosine_p - real_part * sine_p
                ).astype(BF16)
                if step == 0:
                    weight = used[block : block + 1, HALF_X : HALF_X + 1]
                    top = lax.broadcasted_iota(jnp.int32, (16, PIX_BLK), 0) == 0
                    only = imag_part[0:1] * weight
                    lone[0:16, outer] = jnp.where(
                        top, only * middle_cosine[:, lanes], 0.0
                    ).astype(BF16)
                    lone[PIX_BLK : PIX_BLK + 16, outer] = jnp.where(
                        top, only * middle_sine[:, lanes], 0.0
                    ).astype(BF16)
            products[block] = lax.dot_general(
                shift_table[:, columns],
                rotated[:, columns],
                contract_last,
                preferred_element_type=F32,
            )

        if step == 0:
            both = lax.dot_general(
                shift_table[...], lone[...], contract_last, preferred_element_type=F32
            )
            flips = (lax.broadcasted_iota(jnp.int32, (NY, PIX_BLK), 0) & 1) == 0
            one = both[NY : NY + 1, PIX_BLK:]
            lone_out[0] = both[:NY, :PIX_BLK] - jnp.where(flips, one, -one)
            one = both[NY : NY + 1, :PIX_BLK]
            lone_out[1] = both[:NY, PIX_BLK:] + jnp.where(flips, one, -one)

        sums = every_sum[:, step * CHUNK : (step + 1) * CHUNK]
        differences = every_difference[:, step * CHUNK : (step + 1) * CHUNK]
        add_hr = add_hi = add_gr = add_gi = jnp.zeros((1, CHUNK), F32)
        for block in range(BLK_BAND):
            edge_real = products[block, NY : NY + 1, :CHUNK]
            edge_imag = products[block, NY : NY + 1, CHUNK:]
            add_hr = add_hr - differences[block : block + 1] * edge_imag
            add_hi = add_hi + differences[block : block + 1] * edge_real
            add_gr = add_gr - sums[block : block + 1] * edge_imag
            add_gi = add_gi + sums[block : block + 1] * edge_real
        add_hr, add_hi = alternating * add_hr, alternating * add_hi
        add_gr, add_gi = alternating * add_gr, alternating * add_gi

        for x_high in range(GRID_XH):
            for y_at in range(GRID_Y):
                for z_at in range(GRID_Z):
                    start = z_at * 64 + x_high * 32 + y_at * 8
                    rows = slice(start, start + 8)
                    herm_real, herm_imag, anti_real, anti_imag = add_hr, add_hi, add_gr, add_gi
                    for block in range(BLK_BAND):
                        real_part = products[block, rows, :CHUNK]
                        imag_part = products[block, rows, CHUNK:]
                        plus, minus = sums[block : block + 1], differences[block : block + 1]
                        herm_real = herm_real + plus * real_part
                        herm_imag = herm_imag + plus * imag_part
                        anti_real = anti_real + minus * real_part
                        anti_imag = anti_imag + minus * imag_part
                    for band in range(GRID_BAND):
                        tiles = []
                        for part in range(2):
                            if band == 0:
                                whole = herm_imag if part else herm_real
                            else:
                                whole = -anti_real if part else anti_imag
                            for lane in range(0, CHUNK, PIX_BLK):
                                tiles.append(whole[:, lane : lane + PIX_BLK])
                        if step == 0:
                            tiles[len(tiles) // 2] = jnp.where(
                                lane_zero, lone_out[band, rows, :], tiles[len(tiles) // 2]
                            )
                        kept, sent = [], []
                        for left, right in zip(tiles[::2], tiles[1::2]):
                            low = jnp.where(upper_rows, left, pltpu.roll(right, ROWS_DEV, 0))
                            high = jnp.where(upper_rows, pltpu.roll(left, ROWS_DEV, 0), right)
                            kept.append(jnp.where(first_core, low, high))
                            sent.append(jnp.where(first_core, high, low))
                        piece = (x_high * GRID_Y + y_at) * GRID_BAND + band
                        target = z_at * 32 + step * (CHUNK // 16)
                        where = slice(target, target + CHUNK // 16)
                        keep_ref[piece, where, :] = jnp.concatenate(kept, axis=0).astype(BF16)
                        send_ref[piece, where, :] = jnp.concatenate(sent, axis=0).astype(BF16)


def local_part(lists, counts, gradient, table, intens):
    out_shape = jax.ShapeDtypeStruct((PIECES, 32 * GRID_Z, PIX_BLK), BF16)
    vmem = pl.BlockSpec(memory_space=pltpu.VMEM)
    anywhere = pl.BlockSpec(memory_space=pl.ANY)
    return pl.pallas_call(
        local_kernel,
        in_specs=[anywhere] * 5,
        out_specs=[vmem, vmem],
        out_shape=[out_shape, out_shape],
        scratch_shapes=[
            pltpu.VMEM((CAP, NX), jnp.int32),
            pltpu.VMEM((1, NX), jnp.int32),
            pltpu.VMEM((2, PIX_BAND), F32),
            pltpu.VMEM((NX, NX), BF16),
            pltpu.VMEM((NX, DEPTH), BF16),
            pltpu.VMEM((TALL, PIX_BAND), F32),
            pltpu.VMEM((TALL, DEPTH), BF16),
            pltpu.VMEM((2 * CHUNK, DEPTH), BF16),
            pltpu.VMEM((2 * PIX_BLK, DEPTH), BF16),
            pltpu.VMEM((BLK_BAND, TALL, 2 * CHUNK), F32),
            pltpu.VMEM((2, NY, PIX_BLK), F32),
            pltpu.SemaphoreType.DMA((3 + STEPS + BLK_BAND * ROWS_DEV,)),
        ],
        compiler_params=pltpu.CompilerParams(vmem_limit_bytes=48 * 1024 * 1024),
    )(lists, counts, gradient, table, intens)


def plane_kernel(pieces_ref, plane_ref):
    total = pieces_ref[0].astype(F32)
    for source in range(1, PIECES):
        total = total + pieces_ref[source].astype(F32)
    plane_ref[...] = total.astype(BF16)


def plane_part(pieces):
    return pl.pallas_call(
        plane_kernel,
        out_shape=jax.ShapeDtypeStruct((32 * GRID_Z, PIX_BLK), BF16),
        compiler_params=pltpu.CompilerParams(vmem_limit_bytes=32 * 1024 * 1024),
    )(pieces)


def final_kernel(parts_ref, table_ref, image_ref):
    total = parts_ref[0].astype(F32)
    for source in range(1, GRID_Z):
        total = total + parts_ref[source].astype(F32)
    tiles = [total[at : at + ROWS_DEV] for at in range(0, 32, ROWS_DEV)]
    total = jnp.concatenate(tiles, axis=1)
    high = total.astype(BF16)
    low = total - high.astype(F32)
    both = jnp.concatenate([high.astype(F32), low], axis=0).astype(BF16)
    image = jnp.dot(both, table_ref[0], preferred_element_type=F32)
    image = image[:ROWS_DEV] + image[ROWS_DEV:]
    image_ref[0] = image + jnp.dot(high, table_ref[1], preferred_element_type=F32)


def final_part(parts, table):
    return pl.pallas_call(
        final_kernel,
        out_shape=jax.ShapeDtypeStruct((1, ROWS_DEV, NX), F32),
        compiler_params=pltpu.CompilerParams(vmem_limit_bytes=32 * 1024 * 1024),
    )(parts, table)


def body(intens, block_list, block_count, pixel_gradient):
    keep, send = local_part(
        block_list.T, block_count.T, pixel_gradient, jnp.asarray(forward_table()), intens
    )
    received = lax.ppermute(send, "core", [(0, 1), (1, 0)])
    chip = (keep.astype(F32) + received.astype(F32)).astype(BF16)
    pieces = lax.all_to_all(
        chip, ("xh", "y", "band"), split_axis=0, concat_axis=0, tiled=True
    )
    plane = plane_part(pieces).reshape(GRID_Z, 32, PIX_BLK)
    parts = lax.all_to_all(plane, "z", split_axis=0, concat_axis=0, tiled=True)
    return final_part(parts, jnp.asarray(backward_table()))


def solution(mesh):
    grid = Mesh(
        mesh.devices.reshape(GRID_Z, GRID_XH, GRID_Y, GRID_CORE, GRID_BAND),
        ROW_AXES + ("band",),
    )
    return jax.shard_map(
        body,
        mesh=grid,
        in_specs=(P(ROW_AXES, None, "band"), P(None, "band"), P(None, "band"), P(None, "band")),
        out_specs=P("band", ROW_AXES, None),
        check_vma=False,
    )
```

```python
import math

import jax
import jax.numpy as jnp
import ml_dtypes
import numpy as np
from jax import lax
from jax.experimental import pallas as pl
from jax.experimental.pallas import tpu as pltpu
from jax.sharding import Mesh
from jax.sharding import PartitionSpec as P

NX = 1024
NY = 512
PIX_BLK = 128
BLK_BAND = 3
PIX_BAND = PIX_BLK * BLK_BAND
ROWS_DEV = 4
CAP = 2
HALF_X = NX // 2
CHUNK = 256
STEPS = HALF_X // CHUNK
GROUP = ROWS_DEV * PIX_BLK
DEPTH = BLK_BAND * GROUP
TALL = NY + 16
GRID_Z, GRID_XH, GRID_Y, GRID_CORE, GRID_BAND = 8, 2, 4, 2, 2
PIECES = GRID_XH * GRID_Y * GRID_BAND
ROW_AXES = ("z", "xh", "y", "core")
F32, BF16 = jnp.float32, jnp.bfloat16


def forward_table():
    turns = np.outer(np.arange(HALF_X + 1), np.arange(NX)) % NX
    angle = turns.astype(np.float32) * np.float32(2.0 * math.pi / NX)
    norm_factor = np.float32(1.0 / math.sqrt(NX))
    cosine, sine = np.cos(angle) * norm_factor, np.sin(angle) * norm_factor
    lower = -sine[:HALF_X]
    lower[0] = cosine[HALF_X]
    pieces = np.stack(
        [cosine[:HALF_X].reshape(STEPS, CHUNK, NX), lower.reshape(STEPS, CHUNK, NX)], axis=1
    )
    return pieces.reshape(NX, NX).astype(ml_dtypes.bfloat16)


def backward_table():
    turns = np.outer(np.arange(HALF_X + 1), np.arange(NX)) % NX
    angle = turns.astype(np.float64) * (2.0 * math.pi / NX)
    scale = 1.0 / math.sqrt(NX) / math.sqrt(GRID_BAND * CAP * PIX_BLK)
    upper = np.cos(angle[:HALF_X]) * scale
    upper[0] *= 0.5
    lower = -np.sin(angle[:HALF_X]) * scale
    lower[0] = np.cos(angle[HALF_X]) * scale
    pieces = np.stack(
        [upper.reshape(STEPS, CHUNK, NX), lower.reshape(STEPS, CHUNK, NX)], axis=1
    )
    whole = pieces.reshape(NX, NX).astype(np.float32)
    high = whole.astype(ml_dtypes.bfloat16)
    low = (whole - high.astype(np.float32)).astype(ml_dtypes.bfloat16)
    return np.stack([high, low])


def horner(variable, coefficients):
    total = jnp.full_like(variable, coefficients[-1])
    for coefficient in coefficients[-2::-1]:
        total = total * variable + coefficient
    return total


SINE = [(-1.0) ** k / math.factorial(2 * k + 1) for k in range(8)]
COSINE = [(-1.0) ** k / math.factorial(2 * k) for k in range(8)]


def small_sincos(angle):
    square = angle * angle
    return angle * horner(square, SINE), horner(square, COSINE)


def cycles_sincos(cycles):
    cycles = cycles - jnp.round(cycles)
    sine, cosine = small_sincos(cycles * math.pi)
    return 2.0 * sine * cosine, 1.0 - 2.0 * sine * sine


def own_place():
    z_at, x_high, y_at, core = (lax.axis_index(name) for name in ROW_AXES)
    return ((z_at * GRID_XH + x_high) * GRID_Y + y_at) * GRID_CORE + core, core


def local_kernel(
    facts_ref,
    table_hbm,
    intens_hbm,
    keep_ref,
    send_ref,
    values,
    table_ref,
    shift_base,
    shift_ref,
    coarse_ref,
    fine_ref,
    middle_ref,
    masks_ref,
    rotated,
    products,
    copy_sem,
):
    own_row, own_core = own_place()
    table_copies = []
    for step in range(STEPS):
        rows = pl.ds(step * 2 * CHUNK, 2 * CHUNK)
        table_copies.append(
            pltpu.make_async_copy(table_hbm.at[rows], table_ref.at[rows], copy_sem.at[step])
        )
    block_copies = []
    for block in range(BLK_BAND):
        block_copies.append([])
        for row in range(ROWS_DEV):
            block_copies[block].append(
                pltpu.make_async_copy(
                    intens_hbm.at[row, :, pl.ds(block * PIX_BLK, PIX_BLK)],
                    values.at[:, pl.ds(block * GROUP + row * PIX_BLK, PIX_BLK)],
                    copy_sem.at[STEPS + block * ROWS_DEV + row],
                )
            )
    for copy in table_copies[:1] + sum(block_copies, []) + table_copies[1:]:
        copy.start()

    gradient_x = facts_ref[3:4, 0:PIX_BAND]
    gradient_y = facts_ref[4:5, 0:PIX_BAND]
    eights = lax.broadcasted_iota(jnp.int32, (HALF_X // 8, PIX_BAND), 0).astype(F32)
    coarse_ref[0], coarse_ref[1] = cycles_sincos(gradient_x * (eights * (8.0 / NX)))
    units = lax.broadcasted_iota(jnp.int32, (8, PIX_BAND), 0).astype(F32)
    fine_ref[0], fine_ref[1] = cycles_sincos(gradient_x * (units * (1.0 / NX)))
    middle_ref[0:1, :], middle_ref[1:2, :] = cycles_sincos(gradient_x * 0.5)

    block_ids = lax.broadcasted_iota(jnp.int32, (8, NX), 0).astype(F32)
    counts = facts_ref[2:3, :]
    used = ((facts_ref[0:1, :] == block_ids) & (counts > 0.5)) | (
        (facts_ref[1:2, :] == block_ids) & (counts > 1.5)
    )
    used = used.astype(F32)
    place_sum = lax.broadcasted_iota(jnp.int32, (HALF_X, HALF_X), 0) + lax.broadcasted_iota(
        jnp.int32, (HALF_X, HALF_X), 1
    )
    reverse = (place_sum == HALF_X).astype(F32).astype(BF16)
    mirror = jnp.dot(used[:, HALF_X:].astype(BF16), reverse, preferred_element_type=F32)
    lane_first = lax.broadcasted_iota(jnp.int32, (8, HALF_X), 1) == 0
    ahead = used[:, :HALF_X]
    mirror = jnp.where(lane_first, ahead, mirror)
    for sort, rows in enumerate((ahead + mirror, ahead - mirror)):
        columns = rows.T
        for block in range(BLK_BAND):
            masks_ref[sort * BLK_BAND + block] = jnp.broadcast_to(
                columns[:, block : block + 1], (HALF_X, PIX_BLK)
            ).astype(BF16)

    nearest = jnp.round(gradient_y)
    rest = gradient_y - nearest
    sinc = horner(rest * rest, [SINE[k] * math.pi ** (2 * k) for k in range(8)])
    small = rest * (math.pi / NY)
    peak = sinc * (1.0 - small * small * (1.0 / 3.0))
    parity = nearest - 2.0 * jnp.floor(nearest * 0.5)
    lobes = (1.0 - 2.0 * parity) * (rest * math.pi) * sinc * (1.0 / NY)
    sine_g, cosine_g = small_sincos(gradient_y * (math.pi / NY))
    index = lax.broadcasted_iota(jnp.int32, (TALL, PIX_BLK), 0)
    offset = index - (ROWS_DEV - 1) - ROWS_DEV * own_row
    distance = offset.astype(F32)
    folded = distance - NY * jnp.round(distance * (1.0 / NY))
    sine_d, cosine_d = small_sincos(folded * (math.pi / NY))
    row_sign = (1 - 2 * (offset & 1)).astype(F32)
    first_row = lax.broadcasted_iota(jnp.int32, (TALL - NY, PIX_BLK), 0) == 0

    def shift_block(block):
        lanes = slice(block * PIX_BLK, (block + 1) * PIX_BLK)
        upper = (cosine_d * cosine_g[:, lanes] + sine_d * sine_g[:, lanes]) * row_sign
        lower = sine_d * cosine_g[:, lanes] - cosine_d * sine_g[:, lanes]
        turns = (distance - nearest[:, lanes]) * (1.0 / NY)
        at_peak = turns == jnp.round(turns)
        lower = jnp.where(at_peak, 1.0, lower)
        shift_base[:, lanes] = jnp.where(
            at_peak, peak[:, lanes], -lobes[:, lanes] * upper / lower
        )
        for row in range(ROWS_DEV):
            column = block * GROUP + row * PIX_BLK
            start = ROWS_DEV - 1 - row
            shift_ref[0:NY, column : column + PIX_BLK] = shift_base[
                start : start + NY, lanes
            ].astype(BF16)
            shift_ref[NY:TALL, column : column + PIX_BLK] = jnp.where(
                first_row, lobes[:, lanes] * (1.0 - 2.0 * (row % 2)), 0.0
            ).astype(BF16)

    even = (lax.broadcasted_iota(jnp.int32, (8, 2 * CHUNK), 0) & 1) == 0
    upper_rows = lax.broadcasted_iota(jnp.int32, (8, PIX_BLK), 0) < ROWS_DEV
    first_core = jnp.full((8, PIX_BLK), own_core, jnp.int32) == 0
    contract_last = (((1,), (1,)), ((), ()))
    height = CHUNK // 16

    for step in range(STEPS):
        table_copies[step].wait()
        table = table_ref[step * 2 * CHUNK : (step + 1) * 2 * CHUNK, :]
        for block in range(BLK_BAND):
            lanes = slice(block * PIX_BLK, (block + 1) * PIX_BLK)
            if step == 0:
                for copy in block_copies[block]:
                    copy.wait()
            spectrum = jnp.dot(
                table,
                values[:, block * GROUP : (block + 1) * GROUP],
                preferred_element_type=F32,
            )
            if step == 0:
                shift_block(block)
            spectrum = spectrum.astype(BF16).astype(F32)
            fine_sine, fine_cosine = fine_ref[0, :, lanes], fine_ref[1, :, lanes]
            sines, cosines = [], []
            for octet in range(step * CHUNK // 8, (step + 1) * CHUNK // 8):
                sine_c = coarse_ref[0, octet : octet + 1, lanes]
                cosine_c = coarse_ref[1, octet : octet + 1, lanes]
                sines.append(sine_c * fine_cosine + cosine_c * fine_sine)
                cosines.append(cosine_c * fine_cosine - sine_c * fine_sine)
            sine_p = jnp.concatenate(sines, axis=0)
            cosine_p = jnp.concatenate(cosines, axis=0)
            plus = masks_ref[block, step * CHUNK : (step + 1) * CHUNK]
            minus = masks_ref[BLK_BAND + block, step * CHUNK : (step + 1) * CHUNK]
            for row in range(ROWS_DEV):
                inner = slice(row * PIX_BLK, (row + 1) * PIX_BLK)
                outer = slice(
                    block * GROUP + row * PIX_BLK, block * GROUP + (row + 1) * PIX_BLK
                )
                real_part = spectrum[:CHUNK, inner]
                imag_part = spectrum[CHUNK:, inner]
                turned_real = (real_part * cosine_p + imag_part * sine_p).astype(BF16)
                turned_imag = (imag_part * cosine_p - real_part * sine_p).astype(BF16)
                rotated[0:CHUNK, outer] = turned_real * plus
                rotated[CHUNK : 2 * CHUNK, outer] = turned_imag * plus
                rotated[2 * CHUNK : 3 * CHUNK, outer] = turned_imag * minus
                rotated[3 * CHUNK :, outer] = -turned_real * minus
                if step == 0:
                    only = imag_part[0:1] * used[block : block + 1, HALF_X : HALF_X + 1]
                    top = lax.broadcasted_iota(jnp.int32, (16, PIX_BLK), 0) == 0
                    for start, which in ((CHUNK, 1), (3 * CHUNK, 0)):
                        old = rotated[start : start + 16, outer].astype(F32)
                        rotated[start : start + 16, outer] = jnp.where(
                            top, only * middle_ref[which : which + 1, lanes], old
                        ).astype(BF16)

        products[...] = lax.dot_general(
            shift_ref[...], rotated[...], contract_last, preferred_element_type=F32
        )
        edge_herm = products[NY : NY + 1, : 2 * CHUNK]
        edge_anti = products[NY : NY + 1, 2 * CHUNK :]
        edges = (
            jnp.where(even, -edge_anti, edge_anti),
            jnp.where(even, edge_herm, -edge_herm),
        )
        for x_high in range(GRID_XH):
            for y_at in range(GRID_Y):
                for z_at in range(GRID_Z):
                    start = z_at * 64 + x_high * 32 + y_at * 8
                    for band in range(GRID_BAND):
                        slots = slice(band * 2 * CHUNK, (band + 1) * 2 * CHUNK)
                        whole = products[start : start + 8, slots] + edges[band]
                        kept, sent = [], []
                        for lane in range(0, 2 * CHUNK, 2 * PIX_BLK):
                            left = whole[:, lane : lane + PIX_BLK]
                            right = whole[:, lane + PIX_BLK : lane + 2 * PIX_BLK]
                            low = jnp.where(upper_rows, left, pltpu.roll(right, ROWS_DEV, 0))
                            high = jnp.where(upper_rows, pltpu.roll(left, ROWS_DEV, 0), right)
                            kept.append(jnp.where(first_core, low, high))
                            sent.append(jnp.where(first_core, high, low))
                        piece = (x_high * GRID_Y + y_at) * GRID_BAND + band
                        target = z_at * 32 + step * height
                        where = slice(target, target + height)
                        keep_ref[piece, where, :] = jnp.concatenate(kept, axis=0).astype(BF16)
                        send_ref[piece, where, :] = jnp.concatenate(sent, axis=0).astype(BF16)


VMEM_SPEC = pl.BlockSpec(memory_space=pltpu.VMEM)
HBM_SPEC = pl.BlockSpec(memory_space=pltpu.HBM)
LOCAL_VMEM = 50 * 1024 * 1024


def local_part(facts, table, intens):
    out_shape = jax.ShapeDtypeStruct((PIECES, 32 * GRID_Z, PIX_BLK), BF16)
    return pl.pallas_call(
        local_kernel,
        in_specs=[VMEM_SPEC, HBM_SPEC, HBM_SPEC],
        out_specs=[VMEM_SPEC] * 2,
        out_shape=[out_shape, out_shape],
        scratch_shapes=[
            pltpu.VMEM((NX, DEPTH), BF16),
            pltpu.VMEM((NX, NX), BF16),
            pltpu.VMEM((TALL, PIX_BAND), F32),
            pltpu.VMEM((TALL, DEPTH), BF16),
            pltpu.VMEM((2, HALF_X // 8, PIX_BAND), F32),
            pltpu.VMEM((2, 8, PIX_BAND), F32),
            pltpu.VMEM((2, PIX_BAND), F32),
            pltpu.VMEM((2 * BLK_BAND, HALF_X, PIX_BLK), BF16),
            pltpu.VMEM((4 * CHUNK, DEPTH), BF16),
            pltpu.VMEM((TALL, 4 * CHUNK), F32),
            pltpu.SemaphoreType.DMA((STEPS + BLK_BAND * ROWS_DEV,)),
        ],
        compiler_params=pltpu.CompilerParams(vmem_limit_bytes=LOCAL_VMEM),
    )(facts, table, intens)


def plane_kernel(pieces_ref, plane_ref):
    total = pieces_ref[0].astype(F32)
    for source in range(1, PIECES):
        total = total + pieces_ref[source].astype(F32)
    plane_ref[...] = total.astype(BF16)


def plane_part(pieces):
    return pl.pallas_call(
        plane_kernel,
        in_specs=[VMEM_SPEC],
        out_specs=VMEM_SPEC,
        out_shape=jax.ShapeDtypeStruct((32 * GRID_Z, PIX_BLK), BF16),
        compiler_params=pltpu.CompilerParams(vmem_limit_bytes=32 * 1024 * 1024),
    )(pieces)


def final_kernel(parts_ref, table_ref, image_ref):
    total = parts_ref[0].astype(F32)
    for source in range(1, GRID_Z):
        total = total + parts_ref[source].astype(F32)
    tiles = [total[at : at + ROWS_DEV] for at in range(0, 32, ROWS_DEV)]
    total = jnp.concatenate(tiles, axis=1)
    high = total.astype(BF16)
    low = total - high.astype(F32)
    both = jnp.concatenate([high.astype(F32), low], axis=0).astype(BF16)
    image = jnp.dot(both, table_ref[0], preferred_element_type=F32)
    image = image[:ROWS_DEV] + image[ROWS_DEV:]
    image_ref[0] = image + jnp.dot(high, table_ref[1], preferred_element_type=F32)


def final_part(parts, table):
    return pl.pallas_call(
        final_kernel,
        in_specs=[VMEM_SPEC] * 2,
        out_specs=VMEM_SPEC,
        out_shape=jax.ShapeDtypeStruct((1, ROWS_DEV, NX), F32),
        compiler_params=pltpu.CompilerParams(vmem_limit_bytes=32 * 1024 * 1024),
    )(parts, table)


def body(intens, block_list, block_count, pixel_gradient):
    facts = jnp.concatenate(
        [
            block_list.T.astype(F32),
            block_count.T.astype(F32),
            jnp.pad(pixel_gradient, ((0, 3), (0, NX - PIX_BAND))),
        ],
        axis=0,
    )
    keep, send = local_part(facts, jnp.asarray(forward_table()), intens)
    received = lax.ppermute(send, "core", [(0, 1), (1, 0)])
    chip = (keep.astype(F32) + received.astype(F32)).astype(BF16)
    pieces = lax.all_to_all(
        chip, ("xh", "y", "band"), split_axis=0, concat_axis=0, tiled=True
    )
    plane = plane_part(pieces).reshape(GRID_Z, 32, PIX_BLK)
    parts = lax.all_to_all(plane, "z", split_axis=0, concat_axis=0, tiled=True)
    return final_part(parts, jnp.asarray(backward_table()))


def solution(mesh):
    grid = Mesh(
        mesh.devices.reshape(GRID_Z, GRID_XH, GRID_Y, GRID_CORE, GRID_BAND),
        ROW_AXES + ("band",),
    )
    return jax.shard_map(
        body,
        mesh=grid,
        in_specs=(P(ROW_AXES, None, "band"), P(None, "band"), P(None, "band"), P(None, "band")),
        out_specs=P("band", ROW_AXES, None),
        check_vma=False,
    )
```

```python
import math

import jax
import jax.numpy as jnp
import ml_dtypes
import numpy as np
from jax import lax
from jax.experimental import pallas as pl
from jax.experimental.pallas import tpu as pltpu
from jax.sharding import Mesh
from jax.sharding import PartitionSpec as P

NX = 1024
NY = 512
PIX_BLK = 128
BLK_BAND = 3
PIX_BAND = PIX_BLK * BLK_BAND
ROWS_DEV = 4
CAP = 2
HALF_X = NX // 2
CHUNK = 256
STEPS = HALF_X // CHUNK
GROUP = ROWS_DEV * PIX_BLK
DEPTH = BLK_BAND * GROUP
TALL = NY + 16
GRID_Z, GRID_XH, GRID_Y, GRID_CORE, GRID_BAND = 8, 2, 4, 2, 2
PIECES = GRID_XH * GRID_Y * GRID_BAND
ROW_AXES = ("z", "xh", "y", "core")
F32, BF16 = jnp.float32, jnp.bfloat16


def forward_table():
    turns = np.outer(np.arange(HALF_X + 1), np.arange(NX)) % NX
    angle = turns.astype(np.float32) * np.float32(2.0 * math.pi / NX)
    norm_factor = np.float32(1.0 / math.sqrt(NX))
    cosine, sine = np.cos(angle) * norm_factor, np.sin(angle) * norm_factor
    lower = -sine[:HALF_X]
    lower[0] = cosine[HALF_X]
    pieces = np.stack(
        [cosine[:HALF_X].reshape(STEPS, CHUNK, NX), lower.reshape(STEPS, CHUNK, NX)], axis=1
    )
    return pieces.reshape(NX, NX).astype(ml_dtypes.bfloat16)


def backward_table():
    turns = np.outer(np.arange(HALF_X + 1), np.arange(NX)) % NX
    angle = turns.astype(np.float64) * (2.0 * math.pi / NX)
    scale = 1.0 / math.sqrt(NX) / math.sqrt(GRID_BAND * CAP * PIX_BLK)
    upper = np.cos(angle[:HALF_X]) * scale
    upper[0] *= 0.5
    lower = -np.sin(angle[:HALF_X]) * scale
    lower[0] = np.cos(angle[HALF_X]) * scale
    pieces = np.stack(
        [upper.reshape(STEPS, CHUNK, NX), lower.reshape(STEPS, CHUNK, NX)], axis=1
    )
    whole = pieces.reshape(NX, NX).astype(np.float32)
    high = whole.astype(ml_dtypes.bfloat16)
    low = (whole - high.astype(np.float32)).astype(ml_dtypes.bfloat16)
    return np.stack([high, low])


def horner(variable, coefficients):
    total = jnp.full_like(variable, coefficients[-1])
    for coefficient in coefficients[-2::-1]:
        total = total * variable + coefficient
    return total


SINE = [(-1.0) ** k / math.factorial(2 * k + 1) for k in range(8)]
COSINE = [(-1.0) ** k / math.factorial(2 * k) for k in range(8)]


def small_sincos(angle):
    square = angle * angle
    return angle * horner(square, SINE), horner(square, COSINE)


def cycles_sincos(cycles):
    cycles = cycles - jnp.round(cycles)
    sine, cosine = small_sincos(cycles * math.pi)
    return 2.0 * sine * cosine, 1.0 - 2.0 * sine * sine


def own_place():
    z_at, x_high, y_at, core = (lax.axis_index(name) for name in ROW_AXES)
    return ((z_at * GRID_XH + x_high) * GRID_Y + y_at) * GRID_CORE + core, core


def local_kernel(
    lists_hbm,
    counts_hbm,
    gradient_hbm,
    table_hbm,
    intens_hbm,
    keep_ref,
    send_ref,
    lists_ref,
    counts_ref,
    gradient_ref,
    values,
    table_ref,
    shift_base,
    shift_ref,
    coarse_ref,
    fine_ref,
    middle_ref,
    masks_ref,
    middle_used,
    rotated,
    products,
    copy_sem,
):
    own_row, own_core = own_place()
    small_copies = [
        pltpu.make_async_copy(gradient_hbm, gradient_ref, copy_sem.at[0]),
        pltpu.make_async_copy(lists_hbm, lists_ref, copy_sem.at[1]),
        pltpu.make_async_copy(counts_hbm, counts_ref, copy_sem.at[2]),
    ]
    table_copies = []
    for step in range(STEPS):
        rows = pl.ds(step * 2 * CHUNK, 2 * CHUNK)
        table_copies.append(
            pltpu.make_async_copy(table_hbm.at[rows], table_ref.at[rows], copy_sem.at[3 + step])
        )
    block_copies = []
    for block in range(BLK_BAND):
        block_copies.append([])
        for row in range(ROWS_DEV):
            block_copies[block].append(
                pltpu.make_async_copy(
                    intens_hbm.at[row, :, pl.ds(block * PIX_BLK, PIX_BLK)],
                    values.at[:, pl.ds(block * GROUP + row * PIX_BLK, PIX_BLK)],
                    copy_sem.at[3 + STEPS + block * ROWS_DEV + row],
                )
            )
    for copy in small_copies + table_copies[:1] + sum(block_copies, []) + table_copies[1:]:
        copy.start()
    for copy in small_copies:
        copy.wait()

    gradient_x = gradient_ref[0:1, :]
    gradient_y = gradient_ref[1:2, :]
    eights = lax.broadcasted_iota(jnp.int32, (HALF_X // 8, PIX_BAND), 0).astype(F32)
    coarse_ref[0], coarse_ref[1] = cycles_sincos(gradient_x * (eights * (8.0 / NX)))
    units = lax.broadcasted_iota(jnp.int32, (8, PIX_BAND), 0).astype(F32)
    fine_ref[0], fine_ref[1] = cycles_sincos(gradient_x * (units * (1.0 / NX)))
    middle_ref[0:1, :], middle_ref[1:2, :] = cycles_sincos(gradient_x * 0.5)

    def make_masks():
        block_ids = lax.broadcasted_iota(jnp.int32, (8, NX), 0)
        counts = counts_ref[0:1, :]
        used = ((lists_ref[0:1, :] == block_ids) & (counts > 0)) | (
            (lists_ref[1:2, :] == block_ids) & (counts > 1)
        )
        used = used.astype(F32)
        place_sum = lax.broadcasted_iota(
            jnp.int32, (HALF_X, HALF_X), 0
        ) + lax.broadcasted_iota(jnp.int32, (HALF_X, HALF_X), 1)
        reverse = (place_sum == HALF_X).astype(F32).astype(BF16)
        mirror = jnp.dot(
            used[:, HALF_X:].astype(BF16), reverse, preferred_element_type=F32
        )
        lane_first = lax.broadcasted_iota(jnp.int32, (8, HALF_X), 1) == 0
        ahead = used[:, :HALF_X]
        mirror = jnp.where(lane_first, ahead, mirror)
        for sort, rows in enumerate((ahead + mirror, ahead - mirror)):
            columns = rows.T
            for block in range(BLK_BAND):
                masks_ref[sort * BLK_BAND + block] = jnp.broadcast_to(
                    columns[:, block : block + 1], (HALF_X, PIX_BLK)
                ).astype(BF16)
        middle_used[...] = jnp.broadcast_to(used[:, HALF_X : HALF_X + 1], (8, PIX_BLK))

    def shift_block(block):
        lanes = slice(block * PIX_BLK, (block + 1) * PIX_BLK)
        gradient = gradient_y[:, lanes]
        nearest = jnp.round(gradient)
        rest = gradient - nearest
        sinc = horner(rest * rest, [SINE[k] * math.pi ** (2 * k) for k in range(8)])
        small = rest * (math.pi / NY)
        peak = sinc * (1.0 - small * small * (1.0 / 3.0))
        parity = nearest - 2.0 * jnp.floor(nearest * 0.5)
        lobes = (1.0 - 2.0 * parity) * (rest * math.pi) * sinc * (1.0 / NY)
        sine_g, cosine_g = small_sincos(gradient * (math.pi / NY))
        index = lax.broadcasted_iota(jnp.int32, (TALL, PIX_BLK), 0)
        offset = index - (ROWS_DEV - 1) - ROWS_DEV * own_row
        distance = offset.astype(F32)
        folded = distance - NY * jnp.round(distance * (1.0 / NY))
        sine_d, cosine_d = small_sincos(folded * (math.pi / NY))
        row_sign = (1 - 2 * (offset & 1)).astype(F32)
        first_row = lax.broadcasted_iota(jnp.int32, (TALL - NY, PIX_BLK), 0) == 0
        upper = (cosine_d * cosine_g + sine_d * sine_g) * row_sign
        lower = sine_d * cosine_g - cosine_d * sine_g
        turns = (distance - nearest) * (1.0 / NY)
        at_peak = turns == jnp.round(turns)
        lower = jnp.where(at_peak, 1.0, lower)
        shift_base[:, lanes] = jnp.where(at_peak, peak, -lobes * upper / lower)
        for row in range(ROWS_DEV):
            column = block * GROUP + row * PIX_BLK
            start = ROWS_DEV - 1 - row
            shift_ref[0:NY, column : column + PIX_BLK] = shift_base[
                start : start + NY, lanes
            ].astype(BF16)
            shift_ref[NY:TALL, column : column + PIX_BLK] = jnp.where(
                first_row, lobes * (1.0 - 2.0 * (row % 2)), 0.0
            ).astype(BF16)

    def transform(step, block):
        return jnp.dot(
            table_ref[step * 2 * CHUNK : (step + 1) * 2 * CHUNK, :],
            values[:, block * GROUP : (block + 1) * GROUP],
            preferred_element_type=F32,
        )

    def rotate(step, block, spectrum):
        lanes = slice(block * PIX_BLK, (block + 1) * PIX_BLK)
        spectrum = spectrum.astype(BF16).astype(F32)
        fine_sine, fine_cosine = fine_ref[0, :, lanes], fine_ref[1, :, lanes]
        sines, cosines = [], []
        for octet in range(step * CHUNK // 8, (step + 1) * CHUNK // 8):
            sine_c = coarse_ref[0, octet : octet + 1, lanes]
            cosine_c = coarse_ref[1, octet : octet + 1, lanes]
            sines.append(sine_c * fine_cosine + cosine_c * fine_sine)
            cosines.append(cosine_c * fine_cosine - sine_c * fine_sine)
        sine_p = jnp.concatenate(sines, axis=0)
        cosine_p = jnp.concatenate(cosines, axis=0)
        plus = masks_ref[block, step * CHUNK : (step + 1) * CHUNK]
        minus = masks_ref[BLK_BAND + block, step * CHUNK : (step + 1) * CHUNK]
        for row in range(ROWS_DEV):
            inner = slice(row * PIX_BLK, (row + 1) * PIX_BLK)
            outer = slice(block * GROUP + row * PIX_BLK, block * GROUP + (row + 1) * PIX_BLK)
            real_part = spectrum[:CHUNK, inner]
            imag_part = spectrum[CHUNK:, inner]
            turned_real = (real_part * cosine_p + imag_part * sine_p).astype(BF16)
            turned_imag = (imag_part * cosine_p - real_part * sine_p).astype(BF16)
            rotated[step, 0:CHUNK, outer] = turned_real * plus
            rotated[step, CHUNK : 2 * CHUNK, outer] = turned_imag * plus
            rotated[step, 2 * CHUNK : 3 * CHUNK, outer] = turned_imag * minus
            rotated[step, 3 * CHUNK :, outer] = -turned_real * minus
            if step == 0:
                only = imag_part[0:1] * middle_used[block : block + 1, :]
                top = lax.broadcasted_iota(jnp.int32, (16, PIX_BLK), 0) == 0
                for start, which in ((CHUNK, 1), (3 * CHUNK, 0)):
                    old = rotated[step, start : start + 16, outer].astype(F32)
                    rotated[step, start : start + 16, outer] = jnp.where(
                        top, only * middle_ref[which : which + 1, lanes], old
                    ).astype(BF16)

    def multiply(step, rows):
        products[step, rows, :] = lax.dot_general(
            shift_ref[rows, :],
            rotated[step],
            (((1,), (1,)), ((), ())),
            preferred_element_type=F32,
        )

    even = (lax.broadcasted_iota(jnp.int32, (8, 2 * CHUNK), 0) & 1) == 0
    upper_rows = lax.broadcasted_iota(jnp.int32, (8, PIX_BLK), 0) < ROWS_DEV
    first_core = jnp.full((8, PIX_BLK), own_core, jnp.int32) == 0
    height = CHUNK // 16

    def store(step, z_range):
        edge_herm = products[step, NY : NY + 1, : 2 * CHUNK]
        edge_anti = products[step, NY : NY + 1, 2 * CHUNK :]
        edges = (
            jnp.where(even, -edge_anti, edge_anti),
            jnp.where(even, edge_herm, -edge_herm),
        )
        for z_at in z_range:
            for x_high in range(GRID_XH):
                for y_at in range(GRID_Y):
                    start = z_at * 64 + x_high * 32 + y_at * 8
                    for band in range(GRID_BAND):
                        slots = slice(band * 2 * CHUNK, (band + 1) * 2 * CHUNK)
                        whole = products[step, start : start + 8, slots] + edges[band]
                        kept, sent = [], []
                        for lane in range(0, 2 * CHUNK, 2 * PIX_BLK):
                            left = whole[:, lane : lane + PIX_BLK]
                            right = whole[:, lane + PIX_BLK : lane + 2 * PIX_BLK]
                            low = jnp.where(upper_rows, left, pltpu.roll(right, ROWS_DEV, 0))
                            high = jnp.where(upper_rows, pltpu.roll(left, ROWS_DEV, 0), right)
                            kept.append(jnp.where(first_core, low, high))
                            sent.append(jnp.where(first_core, high, low))
                        piece = (x_high * GRID_Y + y_at) * GRID_BAND + band
                        target = z_at * 32 + step * height
                        where = slice(target, target + height)
                        keep_ref[piece, where, :] = jnp.concatenate(kept, axis=0)
                        send_ref[piece, where, :] = jnp.concatenate(sent, axis=0).astype(BF16)

    def wait_for(copies):
        for copy in copies:
            copy.wait()

    wait_for(table_copies[:1] + block_copies[0])
    spectrum = transform(0, 0)
    make_masks()
    rotate(0, 0, spectrum)
    wait_for(block_copies[1])
    spectrum = transform(0, 1)
    shift_block(0)
    rotate(0, 1, spectrum)
    wait_for(block_copies[2] + table_copies[1:])
    spectrum = transform(0, 2)
    shift_block(1)
    rotate(0, 2, spectrum)
    spectrum = transform(1, 0)
    shift_block(2)
    rotate(1, 0, spectrum)
    spectrum = transform(1, 1)
    rotate(1, 1, spectrum)
    spectrum = transform(1, 2)
    multiply(0, slice(NY // 2, TALL))
    rotate(1, 2, spectrum)
    multiply(0, slice(0, NY // 2))
    store(0, range(GRID_Z // 2, GRID_Z))
    multiply(1, slice(NY // 2, TALL))
    store(0, range(GRID_Z // 2))
    multiply(1, slice(0, NY // 2))
    store(1, range(GRID_Z // 2, GRID_Z))
    store(1, range(GRID_Z // 2))


VMEM_SPEC = pl.BlockSpec(memory_space=pltpu.VMEM)
HBM_SPEC = pl.BlockSpec(memory_space=pltpu.HBM)
LOCAL_VMEM = 50 * 1024 * 1024


def local_part(lists, counts, gradient, table, intens):
    shape = (PIECES, 32 * GRID_Z, PIX_BLK)
    return pl.pallas_call(
        local_kernel,
        in_specs=[HBM_SPEC] * 5,
        out_specs=[VMEM_SPEC] * 2,
        out_shape=[jax.ShapeDtypeStruct(shape, F32), jax.ShapeDtypeStruct(shape, BF16)],
        scratch_shapes=[
            pltpu.VMEM((CAP, NX), jnp.int32),
            pltpu.VMEM((1, NX), jnp.int32),
            pltpu.VMEM((2, PIX_BAND), F32),
            pltpu.VMEM((NX, DEPTH), BF16),
            pltpu.VMEM((NX, NX), BF16),
            pltpu.VMEM((TALL, PIX_BAND), F32),
            pltpu.VMEM((TALL, DEPTH), BF16),
            pltpu.VMEM((2, HALF_X // 8, PIX_BAND), F32),
            pltpu.VMEM((2, 8, PIX_BAND), F32),
            pltpu.VMEM((2, PIX_BAND), F32),
            pltpu.VMEM((2 * BLK_BAND, HALF_X, PIX_BLK), BF16),
            pltpu.VMEM((8, PIX_BLK), F32),
            pltpu.VMEM((STEPS, 4 * CHUNK, DEPTH), BF16),
            pltpu.VMEM((STEPS, TALL, 4 * CHUNK), F32),
            pltpu.SemaphoreType.DMA((3 + STEPS + BLK_BAND * ROWS_DEV,)),
        ],
        compiler_params=pltpu.CompilerParams(vmem_limit_bytes=LOCAL_VMEM),
    )(lists, counts, gradient, table, intens)


def plane_kernel(pieces_ref, plane_ref):
    total = pieces_ref[0].astype(F32)
    for source in range(1, PIECES):
        total = total + pieces_ref[source].astype(F32)
    plane_ref[...] = total.astype(BF16)


def plane_part(pieces):
    return pl.pallas_call(
        plane_kernel,
        in_specs=[VMEM_SPEC],
        out_specs=VMEM_SPEC,
        out_shape=jax.ShapeDtypeStruct((32 * GRID_Z, PIX_BLK), BF16),
        compiler_params=pltpu.CompilerParams(vmem_limit_bytes=32 * 1024 * 1024),
    )(pieces)


def final_kernel(parts_ref, table_ref, image_ref):
    total = parts_ref[0].astype(F32)
    for source in range(1, GRID_Z):
        total = total + parts_ref[source].astype(F32)
    tiles = [total[at : at + ROWS_DEV] for at in range(0, 32, ROWS_DEV)]
    total = jnp.concatenate(tiles, axis=1)
    high = total.astype(BF16)
    low = total - high.astype(F32)
    both = jnp.concatenate([high.astype(F32), low], axis=0).astype(BF16)
    image = jnp.dot(both, table_ref[0], preferred_element_type=F32)
    image = image[:ROWS_DEV] + image[ROWS_DEV:]
    image_ref[0] = image + jnp.dot(high, table_ref[1], preferred_element_type=F32)


def final_part(parts, table):
    return pl.pallas_call(
        final_kernel,
        in_specs=[VMEM_SPEC] * 2,
        out_specs=VMEM_SPEC,
        out_shape=jax.ShapeDtypeStruct((1, ROWS_DEV, NX), F32),
        compiler_params=pltpu.CompilerParams(vmem_limit_bytes=32 * 1024 * 1024),
    )(parts, table)


def body(intens, block_list, block_count, pixel_gradient):
    keep, send = local_part(
        block_list.T, block_count.T, pixel_gradient, jnp.asarray(forward_table()), intens
    )
    received = lax.ppermute(send, "core", [(0, 1), (1, 0)])
    chip = (keep + received.astype(F32)).astype(BF16)
    pieces = lax.all_to_all(
        chip, ("xh", "y", "band"), split_axis=0, concat_axis=0, tiled=True
    )
    plane = plane_part(pieces).reshape(GRID_Z, 32, PIX_BLK)
    parts = lax.all_to_all(plane, "z", split_axis=0, concat_axis=0, tiled=True)
    return final_part(parts, jnp.asarray(backward_table()))


def solution(mesh):
    grid = Mesh(
        mesh.devices.reshape(GRID_Z, GRID_XH, GRID_Y, GRID_CORE, GRID_BAND),
        ROW_AXES + ("band",),
    )
    return jax.shard_map(
        body,
        mesh=grid,
        in_specs=(P(ROW_AXES, None, "band"), P(None, "band"), P(None, "band"), P(None, "band")),
        out_specs=P("band", ROW_AXES, None),
        check_vma=False,
    )
```

```python
import math

import jax
import jax.numpy as jnp
import ml_dtypes
import numpy as np
from jax import lax
from jax.experimental import pallas as pl
from jax.experimental.pallas import tpu as pltpu
from jax.sharding import Mesh
from jax.sharding import PartitionSpec as P

NX = 1024
NY = 512
PIX_BLK = 128
BLK_BAND = 3
PIX_BAND = PIX_BLK * BLK_BAND
ROWS_DEV = 4
CAP = 2
HALF_X = NX // 2
CHUNK = 256
STEPS = HALF_X // CHUNK
GROUP = ROWS_DEV * PIX_BLK
DEPTH = BLK_BAND * GROUP
TALL = NY + 16
GRID_Z, GRID_XH, GRID_Y, GRID_CORE, GRID_BAND = 8, 2, 4, 2, 2
PIECES = GRID_XH * GRID_Y * GRID_BAND
ROW_AXES = ("z", "xh", "y", "core")
F32, BF16 = jnp.float32, jnp.bfloat16


def forward_table():
    turns = np.outer(np.arange(HALF_X + 1), np.arange(NX)) % NX
    angle = turns.astype(np.float32) * np.float32(2.0 * math.pi / NX)
    norm_factor = np.float32(1.0 / math.sqrt(NX))
    cosine, sine = np.cos(angle) * norm_factor, np.sin(angle) * norm_factor
    lower = -sine[:HALF_X]
    lower[0] = cosine[HALF_X]
    pieces = np.stack(
        [cosine[:HALF_X].reshape(STEPS, CHUNK, NX), lower.reshape(STEPS, CHUNK, NX)], axis=1
    )
    return pieces.reshape(NX, NX).astype(ml_dtypes.bfloat16)


def backward_table():
    turns = np.outer(np.arange(HALF_X + 1), np.arange(NX)) % NX
    angle = turns.astype(np.float64) * (2.0 * math.pi / NX)
    scale = 1.0 / math.sqrt(NX) / math.sqrt(GRID_BAND * CAP * PIX_BLK)
    upper = np.cos(angle[:HALF_X]) * scale
    upper[0] *= 0.5
    lower = -np.sin(angle[:HALF_X]) * scale
    lower[0] = np.cos(angle[HALF_X]) * scale
    pieces = np.stack(
        [upper.reshape(STEPS, CHUNK, NX), lower.reshape(STEPS, CHUNK, NX)], axis=1
    )
    whole = pieces.reshape(NX, NX).astype(np.float32)
    high = whole.astype(ml_dtypes.bfloat16)
    low = (whole - high.astype(np.float32)).astype(ml_dtypes.bfloat16)
    return np.stack([high, low])


def horner(variable, coefficients):
    total = jnp.full_like(variable, coefficients[-1])
    for coefficient in coefficients[-2::-1]:
        total = total * variable + coefficient
    return total


SINE = [(-1.0) ** k / math.factorial(2 * k + 1) for k in range(8)]
COSINE = [(-1.0) ** k / math.factorial(2 * k) for k in range(8)]


def small_sincos(angle):
    square = angle * angle
    return angle * horner(square, SINE), horner(square, COSINE)


def cycles_sincos(cycles):
    cycles = cycles - jnp.round(cycles)
    sine, cosine = small_sincos(cycles * math.pi)
    return 2.0 * sine * cosine, 1.0 - 2.0 * sine * sine


def own_place():
    z_at, x_high, y_at, core = (lax.axis_index(name) for name in ROW_AXES)
    return ((z_at * GRID_XH + x_high) * GRID_Y + y_at) * GRID_CORE + core, core


def local_kernel(
    facts_ref,
    table_hbm,
    intens_hbm,
    keep_ref,
    send_ref,
    values,
    table_ref,
    shift_base,
    shift_ref,
    coarse_ref,
    fine_ref,
    middle_ref,
    masks_ref,
    middle_used,
    rotated,
    products,
    copy_sem,
):
    own_row, own_core = own_place()
    table_copies = []
    for step in range(STEPS):
        rows = pl.ds(step * 2 * CHUNK, 2 * CHUNK)
        table_copies.append(
            pltpu.make_async_copy(table_hbm.at[rows], table_ref.at[rows], copy_sem.at[step])
        )
    block_copies = []
    for block in range(BLK_BAND):
        block_copies.append([])
        for row in range(ROWS_DEV):
            block_copies[block].append(
                pltpu.make_async_copy(
                    intens_hbm.at[row, :, pl.ds(block * PIX_BLK, PIX_BLK)],
                    values.at[:, pl.ds(block * GROUP + row * PIX_BLK, PIX_BLK)],
                    copy_sem.at[STEPS + block * ROWS_DEV + row],
                )
            )
    for copy in table_copies[:1] + sum(block_copies, []) + table_copies[1:]:
        copy.start()

    gradient_x = facts_ref[1:2, 0:PIX_BAND]
    gradient_y = facts_ref[2:3, 0:PIX_BAND]
    eights = lax.broadcasted_iota(jnp.int32, (HALF_X // 8, PIX_BAND), 0).astype(F32)
    coarse_ref[0], coarse_ref[1] = cycles_sincos(gradient_x * (eights * (8.0 / NX)))
    units = lax.broadcasted_iota(jnp.int32, (8, PIX_BAND), 0).astype(F32)
    fine_ref[0], fine_ref[1] = cycles_sincos(gradient_x * (units * (1.0 / NX)))
    middle_ref[0:1, :], middle_ref[1:2, :] = cycles_sincos(gradient_x * 0.5)

    def make_masks():
        block_ids = lax.broadcasted_iota(jnp.int32, (8, NX), 0)
        packed = facts_ref[0:1, :].astype(jnp.int32)
        counts = packed >> 4
        used = (((packed & 3) == block_ids) & (counts > 0)) | (
            (((packed >> 2) & 3) == block_ids) & (counts > 1)
        )
        used = used.astype(F32)
        place_sum = lax.broadcasted_iota(
            jnp.int32, (HALF_X, HALF_X), 0
        ) + lax.broadcasted_iota(jnp.int32, (HALF_X, HALF_X), 1)
        reverse = (place_sum == HALF_X).astype(F32).astype(BF16)
        mirror = jnp.dot(
            used[:, HALF_X:].astype(BF16), reverse, preferred_element_type=F32
        )
        lane_first = lax.broadcasted_iota(jnp.int32, (8, HALF_X), 1) == 0
        ahead = used[:, :HALF_X]
        mirror = jnp.where(lane_first, ahead, mirror)
        for sort, rows in enumerate((ahead + mirror, ahead - mirror)):
            columns = rows.T
            for block in range(BLK_BAND):
                masks_ref[sort * BLK_BAND + block] = jnp.broadcast_to(
                    columns[:, block : block + 1], (HALF_X, PIX_BLK)
                ).astype(BF16)
        middle_used[...] = jnp.broadcast_to(used[:, HALF_X : HALF_X + 1], (8, PIX_BLK))

    upper_rows = lax.broadcasted_iota(jnp.int32, (8, PIX_BLK), 0) < ROWS_DEV

    def shift_block(block):
        lanes = slice(block * PIX_BLK, (block + 1) * PIX_BLK)
        gradient = gradient_y[:, lanes]
        nearest = jnp.round(gradient)
        rest = gradient - nearest
        sinc = horner(rest * rest, [SINE[k] * math.pi ** (2 * k) for k in range(8)])
        small = rest * (math.pi / NY)
        peak = sinc * (1.0 - small * small * (1.0 / 3.0))
        parity = nearest - 2.0 * jnp.floor(nearest * 0.5)
        lobes = (1.0 - 2.0 * parity) * (rest * math.pi) * sinc * (1.0 / NY)
        sine_g, cosine_g = small_sincos(gradient * (math.pi / NY))
        first_row = lax.broadcasted_iota(jnp.int32, (TALL - NY, PIX_BLK), 0) == 0
        for row in range(ROWS_DEV):
            column = block * GROUP + row * PIX_BLK
            shift_ref[NY:TALL, column : column + PIX_BLK] = jnp.where(
                first_row, lobes * (1.0 - 2.0 * (row % 2)), 0.0
            ).astype(BF16)
        for half in range(GRID_CORE):
            core = own_core if half == 0 else 1 - own_core
            offset = (
                lax.broadcasted_iota(jnp.int32, (NY, PIX_BLK), 0)
                - (ROWS_DEV - 1)
                + ROWS_DEV * (core - own_row)
            )
            distance = offset.astype(F32)
            folded = distance - NY * jnp.round(distance * (1.0 / NY))
            sine_d, cosine_d = small_sincos(folded * (math.pi / NY))
            row_sign = (1 - 2 * (offset & 1)).astype(F32)
            upper = (cosine_d * cosine_g + sine_d * sine_g) * row_sign
            lower = sine_d * cosine_g - cosine_d * sine_g
            turns = (distance - nearest) * (1.0 / NY)
            at_peak = turns == jnp.round(turns)
            lower = jnp.where(at_peak, 1.0, lower)
            shift_base[...] = jnp.where(at_peak, peak, -lobes * upper / lower)
            for place in range(GRID_XH * GRID_Y):
                for quad in range(GRID_Z // 4):
                    tiles = []
                    for pair in range(2):
                        start = (quad * 4 + pair * 2) * 64 + place * 8
                        tiles.append(
                            (shift_base[start : start + 8, :], shift_base[start + 64 : start + 72, :])
                        )
                    target = half * (NY // 2) + place * 32 + quad * 16
                    for row in range(ROWS_DEV):
                        column = block * GROUP + row * PIX_BLK
                        merged = []
                        for left, right in tiles:
                            if row < ROWS_DEV - 1:
                                left = pltpu.roll(left, 5 + row, 0)
                            merged.append(
                                jnp.where(upper_rows, left, pltpu.roll(right, 1 + row, 0))
                            )
                        shift_ref[target : target + 16, column : column + PIX_BLK] = (
                            jnp.concatenate(merged, axis=0).astype(BF16)
                        )

    def transform(step, block):
        return jnp.dot(
            table_ref[step * 2 * CHUNK : (step + 1) * 2 * CHUNK, :],
            values[:, block * GROUP : (block + 1) * GROUP],
            preferred_element_type=F32,
        )

    def rotate(step, block, spectrum):
        lanes = slice(block * PIX_BLK, (block + 1) * PIX_BLK)
        spectrum = spectrum.astype(BF16).astype(F32)
        fine_sine, fine_cosine = fine_ref[0, :, lanes], fine_ref[1, :, lanes]
        sines, cosines = [], []
        for octet in range(step * CHUNK // 8, (step + 1) * CHUNK // 8):
            sine_c = coarse_ref[0, octet : octet + 1, lanes]
            cosine_c = coarse_ref[1, octet : octet + 1, lanes]
            sines.append(sine_c * fine_cosine + cosine_c * fine_sine)
            cosines.append(cosine_c * fine_cosine - sine_c * fine_sine)
        sine_p = jnp.concatenate(sines, axis=0)
        cosine_p = jnp.concatenate(cosines, axis=0)
        plus = masks_ref[block, step * CHUNK : (step + 1) * CHUNK]
        minus = masks_ref[BLK_BAND + block, step * CHUNK : (step + 1) * CHUNK]
        for row in range(ROWS_DEV):
            inner = slice(row * PIX_BLK, (row + 1) * PIX_BLK)
            outer = slice(block * GROUP + row * PIX_BLK, block * GROUP + (row + 1) * PIX_BLK)
            real_part = spectrum[:CHUNK, inner]
            imag_part = spectrum[CHUNK:, inner]
            turned_real = (real_part * cosine_p + imag_part * sine_p).astype(BF16)
            turned_imag = (imag_part * cosine_p - real_part * sine_p).astype(BF16)
            rotated[step, 0:CHUNK, outer] = turned_real * plus
            rotated[step, CHUNK : 2 * CHUNK, outer] = turned_imag * plus
            rotated[step, 2 * CHUNK : 3 * CHUNK, outer] = turned_imag * minus
            rotated[step, 3 * CHUNK :, outer] = -turned_real * minus
            if step == 0:
                only = imag_part[0:1] * middle_used[block : block + 1, :]
                top = lax.broadcasted_iota(jnp.int32, (16, PIX_BLK), 0) == 0
                for start, which in ((CHUNK, 1), (3 * CHUNK, 0)):
                    old = rotated[step, start : start + 16, outer].astype(F32)
                    rotated[step, start : start + 16, outer] = jnp.where(
                        top, only * middle_ref[which : which + 1, lanes], old
                    ).astype(BF16)

    def multiply(step):
        products[step] = lax.dot_general(
            shift_ref[...],
            rotated[step],
            (((1,), (1,)), ((), ())),
            preferred_element_type=F32,
        )

    even = (lax.broadcasted_iota(jnp.int32, (32, 2 * CHUNK), 0) & 1) == 0

    def store(step):
        edge_herm = products[step, NY : NY + 1, : 2 * CHUNK]
        edge_anti = products[step, NY : NY + 1, 2 * CHUNK :]
        edges = (
            jnp.where(even, -edge_anti, edge_anti),
            jnp.where(even, edge_herm, -edge_herm),
        )
        for half, out_ref in enumerate((keep_ref, send_ref)):
            for place in range(GRID_XH * GRID_Y):
                start = half * (NY // 2) + place * 32
                for band in range(GRID_BAND):
                    slots = slice(band * 2 * CHUNK, (band + 1) * 2 * CHUNK)
                    whole = (products[step, start : start + 32, slots] + edges[band]).astype(
                        out_ref.dtype
                    )
                    for tile in range(2 * CHUNK // PIX_BLK):
                        target = (step * (2 * CHUNK // PIX_BLK) + tile) * 32
                        out_ref[place * GRID_BAND + band, target : target + 32, :] = whole[
                            :, tile * PIX_BLK : (tile + 1) * PIX_BLK
                        ]

    def wait_for(copies):
        for copy in copies:
            copy.wait()

    make_masks()
    for block in range(BLK_BAND):
        shift_block(block)
    wait_for(table_copies[:1] + block_copies[0])
    rotate(0, 0, transform(0, 0))
    wait_for(block_copies[1])
    rotate(0, 1, transform(0, 1))
    wait_for(block_copies[2] + table_copies[1:])
    rotate(0, 2, transform(0, 2))
    multiply(0)
    rotate(1, 0, transform(1, 0))
    rotate(1, 1, transform(1, 1))
    store(0)
    rotate(1, 2, transform(1, 2))
    multiply(1)
    store(1)


VMEM_SPEC = pl.BlockSpec(memory_space=pltpu.VMEM)
HBM_SPEC = pl.BlockSpec(memory_space=pltpu.HBM)
LOCAL_VMEM = 50 * 1024 * 1024


def local_part(facts, table, intens):
    shape = (PIECES, 32 * GRID_Z, PIX_BLK)
    return pl.pallas_call(
        local_kernel,
        in_specs=[VMEM_SPEC, HBM_SPEC, HBM_SPEC],
        out_specs=[VMEM_SPEC] * 2,
        out_shape=[jax.ShapeDtypeStruct(shape, F32), jax.ShapeDtypeStruct(shape, BF16)],
        scratch_shapes=[
            pltpu.VMEM((NX, DEPTH), BF16),
            pltpu.VMEM((NX, NX), BF16),
            pltpu.VMEM((NY, PIX_BLK), F32),
            pltpu.VMEM((TALL, DEPTH), BF16),
            pltpu.VMEM((2, HALF_X // 8, PIX_BAND), F32),
            pltpu.VMEM((2, 8, PIX_BAND), F32),
            pltpu.VMEM((2, PIX_BAND), F32),
            pltpu.VMEM((2 * BLK_BAND, HALF_X, PIX_BLK), BF16),
            pltpu.VMEM((8, PIX_BLK), F32),
            pltpu.VMEM((STEPS, 4 * CHUNK, DEPTH), BF16),
            pltpu.VMEM((STEPS, TALL, 4 * CHUNK), F32),
            pltpu.SemaphoreType.DMA((STEPS + BLK_BAND * ROWS_DEV,)),
        ],
        compiler_params=pltpu.CompilerParams(vmem_limit_bytes=LOCAL_VMEM),
    )(facts, table, intens)


def plane_kernel(pieces_ref, plane_ref):
    total = pieces_ref[0].astype(F32)
    for source in range(1, PIECES):
        total = total + pieces_ref[source].astype(F32)
    for z_at in range(GRID_Z):
        rows = [
            total[tile * 32 + z_at * ROWS_DEV : tile * 32 + (z_at + 1) * ROWS_DEV]
            for tile in range(NX // PIX_BLK)
        ]
        plane_ref[z_at] = jnp.concatenate(rows, axis=0).astype(BF16)


def plane_part(pieces):
    return pl.pallas_call(
        plane_kernel,
        in_specs=[VMEM_SPEC],
        out_specs=VMEM_SPEC,
        out_shape=jax.ShapeDtypeStruct((GRID_Z, 32, PIX_BLK), BF16),
        compiler_params=pltpu.CompilerParams(vmem_limit_bytes=32 * 1024 * 1024),
    )(pieces)


def final_kernel(parts_ref, table_ref, image_ref):
    total = parts_ref[0].astype(F32)
    for source in range(1, GRID_Z):
        total = total + parts_ref[source].astype(F32)
    tiles = [total[at : at + ROWS_DEV] for at in range(0, 32, ROWS_DEV)]
    total = jnp.concatenate(tiles, axis=1)
    high = total.astype(BF16)
    low = total - high.astype(F32)
    both = jnp.concatenate([high.astype(F32), low], axis=0).astype(BF16)
    image = jnp.dot(both, table_ref[0], preferred_element_type=F32)
    image = image[:ROWS_DEV] + image[ROWS_DEV:]
    image_ref[0] = image + jnp.dot(high, table_ref[1], preferred_element_type=F32)


def final_part(parts, table):
    return pl.pallas_call(
        final_kernel,
        in_specs=[VMEM_SPEC] * 2,
        out_specs=VMEM_SPEC,
        out_shape=jax.ShapeDtypeStruct((1, ROWS_DEV, NX), F32),
        compiler_params=pltpu.CompilerParams(vmem_limit_bytes=32 * 1024 * 1024),
    )(parts, table)


def body(intens, block_list, block_count, pixel_gradient):
    packed = block_list[:, 0] + 4 * block_list[:, 1] + 16 * block_count[:, 0]
    facts = jnp.concatenate(
        [
            packed.astype(F32)[None],
            jnp.pad(pixel_gradient, ((0, 5), (0, NX - PIX_BAND))),
        ],
        axis=0,
    )
    keep, send = local_part(facts, jnp.asarray(forward_table()), intens)
    received = lax.ppermute(send, "core", [(0, 1), (1, 0)])
    chip = (keep + received.astype(F32)).astype(BF16)
    pieces = lax.all_to_all(
        chip, ("xh", "y", "band"), split_axis=0, concat_axis=0, tiled=True
    )
    plane = plane_part(pieces)
    parts = lax.all_to_all(plane, "z", split_axis=0, concat_axis=0, tiled=True)
    return final_part(parts, jnp.asarray(backward_table()))


def solution(mesh):
    grid = Mesh(
        mesh.devices.reshape(GRID_Z, GRID_XH, GRID_Y, GRID_CORE, GRID_BAND),
        ROW_AXES + ("band",),
    )
    return jax.shard_map(
        body,
        mesh=grid,
        in_specs=(P(ROW_AXES, None, "band"), P(None, "band"), P(None, "band"), P(None, "band")),
        out_specs=P("band", ROW_AXES, None),
        check_vma=False,
    )
```

```python
import math

import jax
import jax.numpy as jnp
import ml_dtypes
import numpy as np
from jax import lax
from jax.experimental import pallas as pl
from jax.experimental.pallas import tpu as pltpu
from jax.sharding import Mesh
from jax.sharding import PartitionSpec as P

NX = 1024
NY = 512
PIX_BLK = 128
BLK_BAND = 3
PIX_BAND = PIX_BLK * BLK_BAND
ROWS_DEV = 4
CAP = 2
HALF_X = NX // 2
CHUNK = 256
STEPS = HALF_X // CHUNK
GROUP = ROWS_DEV * PIX_BLK
DEPTH = BLK_BAND * GROUP
TALL = NY + 16
GRID_Z, GRID_XH, GRID_Y, GRID_CORE, GRID_BAND = 8, 2, 4, 2, 2
PIECES = GRID_XH * GRID_Y * GRID_BAND
ROW_AXES = ("z", "xh", "y", "core")
F32, BF16 = jnp.float32, jnp.bfloat16


def table_angles():
    freqs = np.concatenate([np.arange(0, HALF_X, 2), np.arange(1, HALF_X, 2)])
    return (np.outer(freqs, np.arange(HALF_X)) % NX) * (2.0 * math.pi / NX)


def stack_parts(upper, lower):
    pieces = [part.reshape(STEPS, CHUNK, HALF_X) for part in (upper, lower)]
    return np.stack(pieces, axis=1).reshape(NX, HALF_X)


def forward_table():
    angle = table_angles()
    upper, lower = np.cos(angle), -np.sin(angle)
    lower[0] = (-1.0) ** np.arange(HALF_X)
    return (stack_parts(upper, lower) / math.sqrt(NX)).astype(ml_dtypes.bfloat16)


def backward_table():
    angle = table_angles()
    upper, lower = np.cos(angle), -np.sin(angle)
    upper[0] *= 0.5
    lower[0] = (-1.0) ** np.arange(HALF_X)
    scale = 1.0 / math.sqrt(NX) / math.sqrt(GRID_BAND * CAP * PIX_BLK)
    whole = (stack_parts(upper, lower) * scale).astype(np.float32)
    high = whole.astype(ml_dtypes.bfloat16)
    low = (whole - high.astype(np.float32)).astype(ml_dtypes.bfloat16)
    return np.stack([high, low])


def horner(variable, coefficients):
    total = jnp.full_like(variable, coefficients[-1])
    for coefficient in coefficients[-2::-1]:
        total = total * variable + coefficient
    return total


SINE = [(-1.0) ** k / math.factorial(2 * k + 1) for k in range(8)]
COSINE = [(-1.0) ** k / math.factorial(2 * k) for k in range(8)]


def small_sincos(angle):
    square = angle * angle
    return angle * horner(square, SINE), horner(square, COSINE)


def cycles_sincos(cycles):
    cycles = cycles - jnp.round(cycles)
    sine, cosine = small_sincos(cycles * math.pi)
    return 2.0 * sine * cosine, 1.0 - 2.0 * sine * sine


def own_place():
    z_at, x_high, y_at, core = (lax.axis_index(name) for name in ROW_AXES)
    return ((z_at * GRID_XH + x_high) * GRID_Y + y_at) * GRID_CORE + core, core


def local_kernel(
    facts_ref,
    table_hbm,
    intens_hbm,
    keep_ref,
    send_ref,
    values,
    folded,
    table_ref,
    shift_base,
    shift_ref,
    coarse_ref,
    fine_ref,
    middle_ref,
    row_facts,
    columns_ref,
    masks_ref,
    middle_used,
    rotated,
    products,
    copy_sem,
):
    own_row, own_core = own_place()
    table_copies = []
    for step in range(STEPS):
        rows = pl.ds(step * 2 * CHUNK, 2 * CHUNK)
        table_copies.append(
            pltpu.make_async_copy(table_hbm.at[rows], table_ref.at[rows], copy_sem.at[step])
        )
    block_copies = []
    for block in range(BLK_BAND):
        block_copies.append([])
        for row in range(ROWS_DEV):
            block_copies[block].append(
                pltpu.make_async_copy(
                    intens_hbm.at[row, :, pl.ds(block * PIX_BLK, PIX_BLK)],
                    values.at[:, pl.ds(block * GROUP + row * PIX_BLK, PIX_BLK)],
                    copy_sem.at[STEPS + block * ROWS_DEV + row],
                )
            )
    for copy in table_copies[:1] + sum(block_copies, []) + table_copies[1:]:
        copy.start()

    gradient_x = facts_ref[1:2, 0:PIX_BAND]
    gradient_y = facts_ref[2:3, 0:PIX_BAND]
    octets = lax.broadcasted_iota(jnp.int32, (CHUNK // 8, PIX_BAND), 0).astype(F32)
    coarse_ref[0], coarse_ref[1] = cycles_sincos(gradient_x * (octets * (16.0 / NX)))
    units = lax.broadcasted_iota(jnp.int32, (8, PIX_BAND), 0).astype(F32) * 2.0
    for step in range(STEPS):
        fine_ref[step, 0], fine_ref[step, 1] = cycles_sincos(
            gradient_x * ((units + step) * (1.0 / NX))
        )
    middle_ref[0:1, :], middle_ref[1:2, :] = cycles_sincos(gradient_x * 0.5)

    def make_masks():
        block_ids = lax.broadcasted_iota(jnp.int32, (8, NX), 0)
        packed = facts_ref[0:1, :].astype(jnp.int32)
        counts = packed >> 4
        used = (((packed & 3) == block_ids) & (counts > 0)) | (
            (((packed >> 2) & 3) == block_ids) & (counts > 1)
        )
        used = used.astype(F32)
        place_sum = lax.broadcasted_iota(
            jnp.int32, (HALF_X, HALF_X), 0
        ) + lax.broadcasted_iota(jnp.int32, (HALF_X, HALF_X), 1)
        reverse = (place_sum == HALF_X).astype(F32).astype(BF16)
        mirror = jnp.dot(
            used[:, HALF_X:].astype(BF16), reverse, preferred_element_type=F32
        )
        lane_first = lax.broadcasted_iota(jnp.int32, (8, HALF_X), 1) == 0
        ahead = used[:, :HALF_X]
        mirror = jnp.where(lane_first, ahead, mirror)
        for sort, rows in enumerate((ahead + mirror, ahead - mirror)):
            columns_ref[sort] = rows.T
            for step in range(STEPS):
                columns = columns_ref[sort, pl.ds(step, CHUNK, stride=2), :]
                for block in range(BLK_BAND):
                    masks_ref[
                        sort * BLK_BAND + block, step * CHUNK : (step + 1) * CHUNK
                    ] = jnp.broadcast_to(
                        columns[:, block : block + 1], (CHUNK, PIX_BLK)
                    ).astype(BF16)
        middle_used[...] = jnp.broadcast_to(used[:, HALF_X : HALF_X + 1], (8, PIX_BLK))

    upper_rows = lax.broadcasted_iota(jnp.int32, (8, PIX_BLK), 0) < ROWS_DEV
    for half in range(GRID_CORE):
        core = own_core if half == 0 else 1 - own_core
        offset = (
            lax.broadcasted_iota(jnp.int32, (NY, PIX_BLK), 0)
            - (ROWS_DEV - 1)
            + ROWS_DEV * (core - own_row)
        )
        distance = offset.astype(F32)
        folded_distance = distance - NY * jnp.round(distance * (1.0 / NY))
        row_facts[half, 0] = distance
        row_facts[half, 1], row_facts[half, 2] = small_sincos(folded_distance * (math.pi / NY))
        row_facts[half, 3] = (1 - 2 * (offset & 1)).astype(F32)

    def shift_block(block):
        lanes = slice(block * PIX_BLK, (block + 1) * PIX_BLK)
        gradient = gradient_y[:, lanes]
        nearest = jnp.round(gradient)
        rest = gradient - nearest
        sinc = horner(rest * rest, [SINE[k] * math.pi ** (2 * k) for k in range(8)])
        small = rest * (math.pi / NY)
        peak = sinc * (1.0 - small * small * (1.0 / 3.0))
        parity = nearest - 2.0 * jnp.floor(nearest * 0.5)
        lobes = (1.0 - 2.0 * parity) * (rest * math.pi) * sinc * (1.0 / NY)
        sine_g, cosine_g = small_sincos(gradient * (math.pi / NY))
        first_row = lax.broadcasted_iota(jnp.int32, (TALL - NY, PIX_BLK), 0) == 0
        for row in range(ROWS_DEV):
            column = block * GROUP + row * PIX_BLK
            shift_ref[NY:TALL, column : column + PIX_BLK] = jnp.where(
                first_row, lobes * (1.0 - 2.0 * (row % 2)), 0.0
            ).astype(BF16)
        for half in range(GRID_CORE):
            distance, sine_d, cosine_d = (row_facts[half, which] for which in range(3))
            row_sign = row_facts[half, 3]
            upper = (cosine_d * cosine_g + sine_d * sine_g) * row_sign
            lower = sine_d * cosine_g - cosine_d * sine_g
            turns = (distance - nearest) * (1.0 / NY)
            at_peak = turns == jnp.round(turns)
            lower = jnp.where(at_peak, 1.0, lower)
            shift_base[...] = jnp.where(at_peak, peak, -lobes * upper / lower)
            for place in range(GRID_XH * GRID_Y):
                for quad in range(GRID_Z // 4):
                    tiles = []
                    for pair in range(2):
                        start = (quad * 4 + pair * 2) * 64 + place * 8
                        tiles.append(
                            (shift_base[start : start + 8, :], shift_base[start + 64 : start + 72, :])
                        )
                    target = half * (NY // 2) + place * 32 + quad * 16
                    for row in range(ROWS_DEV):
                        column = block * GROUP + row * PIX_BLK
                        merged = []
                        for left, right in tiles:
                            if row < ROWS_DEV - 1:
                                left = pltpu.roll(left, 5 + row, 0)
                            merged.append(
                                jnp.where(upper_rows, left, pltpu.roll(right, 1 + row, 0))
                            )
                        shift_ref[target : target + 16, column : column + PIX_BLK] = (
                            jnp.concatenate(merged, axis=0).astype(BF16)
                        )

    def fold(block):
        columns = slice(block * GROUP, (block + 1) * GROUP)
        near, far = values[:HALF_X, columns], values[HALF_X:, columns]
        folded[0, :, columns] = near + far
        folded[1, :, columns] = near - far

    def transform(step, block):
        return jnp.dot(
            table_ref[step * 2 * CHUNK : (step + 1) * 2 * CHUNK, :],
            folded[step, :, block * GROUP : (block + 1) * GROUP],
            preferred_element_type=F32,
        )

    def rotate(step, block, spectrum):
        lanes = slice(block * PIX_BLK, (block + 1) * PIX_BLK)
        spectrum = spectrum.astype(BF16).astype(F32)
        fine_sine, fine_cosine = fine_ref[step, 0, :, lanes], fine_ref[step, 1, :, lanes]
        sines, cosines = [], []
        for octet in range(CHUNK // 8):
            sine_c = coarse_ref[0, octet : octet + 1, lanes]
            cosine_c = coarse_ref[1, octet : octet + 1, lanes]
            sines.append(sine_c * fine_cosine + cosine_c * fine_sine)
            cosines.append(cosine_c * fine_cosine - sine_c * fine_sine)
        sine_p = jnp.concatenate(sines, axis=0)
        cosine_p = jnp.concatenate(cosines, axis=0)
        plus = masks_ref[block, step * CHUNK : (step + 1) * CHUNK]
        minus = masks_ref[BLK_BAND + block, step * CHUNK : (step + 1) * CHUNK]
        for row in range(ROWS_DEV):
            inner = slice(row * PIX_BLK, (row + 1) * PIX_BLK)
            outer = slice(block * GROUP + row * PIX_BLK, block * GROUP + (row + 1) * PIX_BLK)
            real_part = spectrum[:CHUNK, inner]
            imag_part = spectrum[CHUNK:, inner]
            turned_real = (real_part * cosine_p + imag_part * sine_p).astype(BF16)
            turned_imag = (imag_part * cosine_p - real_part * sine_p).astype(BF16)
            rotated[step, 0:CHUNK, outer] = turned_real * plus
            rotated[step, CHUNK : 2 * CHUNK, outer] = turned_imag * plus
            rotated[step, 2 * CHUNK : 3 * CHUNK, outer] = turned_imag * minus
            rotated[step, 3 * CHUNK :, outer] = -turned_real * minus
            if step == 0:
                only = imag_part[0:1] * middle_used[block : block + 1, :]
                top = lax.broadcasted_iota(jnp.int32, (16, PIX_BLK), 0) == 0
                for start, which in ((CHUNK, 1), (3 * CHUNK, 0)):
                    old = rotated[step, start : start + 16, outer].astype(F32)
                    rotated[step, start : start + 16, outer] = jnp.where(
                        top, only * middle_ref[which : which + 1, lanes], old
                    ).astype(BF16)

    def multiply(step):
        products[step] = lax.dot_general(
            shift_ref[...],
            rotated[step],
            (((1,), (1,)), ((), ())),
            preferred_element_type=F32,
        )

    even = (lax.broadcasted_iota(jnp.int32, (32, 2 * CHUNK), 0) & 1) == 0

    def store(step):
        edge_herm = products[step, NY : NY + 1, : 2 * CHUNK]
        edge_anti = products[step, NY : NY + 1, 2 * CHUNK :]
        edges = (
            jnp.where(even, -edge_anti, edge_anti),
            jnp.where(even, edge_herm, -edge_herm),
        )
        for half, out_ref in enumerate((keep_ref, send_ref)):
            for place in range(GRID_XH * GRID_Y):
                start = half * (NY // 2) + place * 32
                for band in range(GRID_BAND):
                    slots = slice(band * 2 * CHUNK, (band + 1) * 2 * CHUNK)
                    whole = (products[step, start : start + 32, slots] + edges[band]).astype(
                        out_ref.dtype
                    )
                    for tile in range(2 * CHUNK // PIX_BLK):
                        target = (step * (2 * CHUNK // PIX_BLK) + tile) * 32
                        out_ref[place * GRID_BAND + band, target : target + 32, :] = whole[
                            :, tile * PIX_BLK : (tile + 1) * PIX_BLK
                        ]

    def wait_for(copies):
        for copy in copies:
            copy.wait()

    make_masks()
    for block in range(BLK_BAND):
        shift_block(block)
    wait_for(table_copies[:1] + block_copies[0])
    fold(0)
    rotate(0, 0, transform(0, 0))
    wait_for(block_copies[1])
    fold(1)
    rotate(0, 1, transform(0, 1))
    wait_for(block_copies[2] + table_copies[1:])
    fold(2)
    rotate(0, 2, transform(0, 2))
    multiply(0)
    rotate(1, 0, transform(1, 0))
    rotate(1, 1, transform(1, 1))
    store(0)
    rotate(1, 2, transform(1, 2))
    multiply(1)
    store(1)


VMEM_SPEC = pl.BlockSpec(memory_space=pltpu.VMEM)
HBM_SPEC = pl.BlockSpec(memory_space=pltpu.HBM)
LOCAL_VMEM = 50 * 1024 * 1024


def local_part(facts, table, intens):
    shape = (PIECES, 32 * GRID_Z, PIX_BLK)
    return pl.pallas_call(
        local_kernel,
        in_specs=[VMEM_SPEC, HBM_SPEC, HBM_SPEC],
        out_specs=[VMEM_SPEC] * 2,
        out_shape=[jax.ShapeDtypeStruct(shape, F32), jax.ShapeDtypeStruct(shape, BF16)],
        scratch_shapes=[
            pltpu.VMEM((NX, DEPTH), BF16),
            pltpu.VMEM((STEPS, HALF_X, DEPTH), BF16),
            pltpu.VMEM((NX, HALF_X), BF16),
            pltpu.VMEM((NY, PIX_BLK), F32),
            pltpu.VMEM((TALL, DEPTH), BF16),
            pltpu.VMEM((2, CHUNK // 8, PIX_BAND), F32),
            pltpu.VMEM((STEPS, 2, 8, PIX_BAND), F32),
            pltpu.VMEM((2, PIX_BAND), F32),
            pltpu.VMEM((GRID_CORE, 4, NY, PIX_BLK), F32),
            pltpu.VMEM((2, HALF_X, 8), F32),
            pltpu.VMEM((2 * BLK_BAND, HALF_X, PIX_BLK), BF16),
            pltpu.VMEM((8, PIX_BLK), F32),
            pltpu.VMEM((STEPS, 4 * CHUNK, DEPTH), BF16),
            pltpu.VMEM((STEPS, TALL, 4 * CHUNK), F32),
            pltpu.SemaphoreType.DMA((STEPS + BLK_BAND * ROWS_DEV,)),
        ],
        compiler_params=pltpu.CompilerParams(vmem_limit_bytes=LOCAL_VMEM),
    )(facts, table, intens)


def plane_kernel(pieces_ref, plane_ref):
    total = pieces_ref[0].astype(F32)
    for source in range(1, PIECES):
        total = total + pieces_ref[source].astype(F32)
    for z_at in range(GRID_Z):
        rows = [
            total[tile * 32 + z_at * ROWS_DEV : tile * 32 + (z_at + 1) * ROWS_DEV]
            for tile in range(NX // PIX_BLK)
        ]
        plane_ref[z_at] = jnp.concatenate(rows, axis=0).astype(BF16)


def plane_part(pieces):
    return pl.pallas_call(
        plane_kernel,
        in_specs=[VMEM_SPEC],
        out_specs=VMEM_SPEC,
        out_shape=jax.ShapeDtypeStruct((GRID_Z, 32, PIX_BLK), BF16),
        compiler_params=pltpu.CompilerParams(vmem_limit_bytes=32 * 1024 * 1024),
    )(pieces)


def final_kernel(parts_ref, table_ref, image_ref):
    total = parts_ref[0].astype(F32)
    for source in range(1, GRID_Z):
        total = total + parts_ref[source].astype(F32)
    tiles = [total[at : at + ROWS_DEV] for at in range(0, 32, ROWS_DEV)]
    total = jnp.concatenate(tiles, axis=1)
    high = total.astype(BF16)
    low = total - high.astype(F32)
    both = jnp.concatenate([high.astype(F32), low], axis=0).astype(BF16)
    halves = []
    for step in range(STEPS):
        slots = slice(step * 2 * CHUNK, (step + 1) * 2 * CHUNK)
        image = jnp.dot(both[:, slots], table_ref[0, slots], preferred_element_type=F32)
        image = image[:ROWS_DEV] + image[ROWS_DEV:]
        halves.append(
            image
            + jnp.dot(high[:, slots], table_ref[1, slots], preferred_element_type=F32)
        )
    image_ref[0, :, :HALF_X] = halves[0] + halves[1]
    image_ref[0, :, HALF_X:] = halves[0] - halves[1]


def final_part(parts, table):
    return pl.pallas_call(
        final_kernel,
        in_specs=[VMEM_SPEC] * 2,
        out_specs=VMEM_SPEC,
        out_shape=jax.ShapeDtypeStruct((1, ROWS_DEV, NX), F32),
        compiler_params=pltpu.CompilerParams(vmem_limit_bytes=32 * 1024 * 1024),
    )(parts, table)


def body(intens, block_list, block_count, pixel_gradient):
    packed = block_list[:, 0] + 4 * block_list[:, 1] + 16 * block_count[:, 0]
    facts = jnp.concatenate(
        [
            packed.astype(F32)[None],
            jnp.pad(pixel_gradient, ((0, 5), (0, NX - PIX_BAND))),
        ],
        axis=0,
    )
    keep, send = local_part(facts, jnp.asarray(forward_table()), intens)
    received = lax.ppermute(send, "core", [(0, 1), (1, 0)])
    chip = (keep + received.astype(F32)).astype(BF16)
    pieces = lax.all_to_all(
        chip, ("xh", "y", "band"), split_axis=0, concat_axis=0, tiled=True
    )
    plane = plane_part(pieces)
    parts = lax.all_to_all(plane, "z", split_axis=0, concat_axis=0, tiled=True)
    return final_part(parts, jnp.asarray(backward_table()))


def solution(mesh):
    grid = Mesh(
        mesh.devices.reshape(GRID_Z, GRID_XH, GRID_Y, GRID_CORE, GRID_BAND),
        ROW_AXES + ("band",),
    )
    return jax.shard_map(
        body,
        mesh=grid,
        in_specs=(P(ROW_AXES, None, "band"), P(None, "band"), P(None, "band"), P(None, "band")),
        out_specs=P("band", ROW_AXES, None),
        check_vma=False,
    )
```

```python
import math

import jax
import jax.numpy as jnp
import ml_dtypes
import numpy as np
from jax import lax
from jax.experimental import pallas as pl
from jax.experimental.pallas import tpu as pltpu
from jax.sharding import Mesh
from jax.sharding import PartitionSpec as P

NX = 1024
NY = 512
PIX_BLK = 128
BLK_BAND = 3
PIX_BAND = PIX_BLK * BLK_BAND
ROWS_DEV = 4
CAP = 2
HALF_X = NX // 2
CHUNK = 256
STEPS = HALF_X // CHUNK
GROUP = ROWS_DEV * PIX_BLK
DEPTH = BLK_BAND * GROUP
TALL = NY + 16
GRID_Z, GRID_XH, GRID_Y, GRID_CORE, GRID_BAND = 8, 2, 4, 2, 2
PIECES = GRID_XH * GRID_Y * GRID_BAND
ROW_AXES = ("z", "xh", "y", "core")
F32, BF16 = jnp.float32, jnp.bfloat16


def forward_table():
    turns = np.outer(np.arange(HALF_X + 1), np.arange(NX)) % NX
    angle = turns.astype(np.float32) * np.float32(2.0 * math.pi / NX)
    norm_factor = np.float32(1.0 / math.sqrt(NX))
    cosine, sine = np.cos(angle) * norm_factor, np.sin(angle) * norm_factor
    lower = -sine[:HALF_X]
    lower[0] = cosine[HALF_X]
    pieces = np.stack(
        [cosine[:HALF_X].reshape(STEPS, CHUNK, NX), lower.reshape(STEPS, CHUNK, NX)], axis=1
    )
    return pieces.reshape(NX, NX).astype(ml_dtypes.bfloat16)


def backward_table():
    turns = np.outer(np.arange(HALF_X + 1), np.arange(HALF_X)) % NX
    angle = turns.astype(np.float64) * (2.0 * math.pi / NX)
    scale = 1.0 / math.sqrt(NX) / math.sqrt(GRID_BAND * CAP * PIX_BLK)
    upper = np.cos(angle[:HALF_X]) * scale
    upper[0] *= 0.5
    lower = -np.sin(angle[:HALF_X]) * scale
    lower[0] = np.cos(angle[HALF_X]) * scale
    pieces = np.stack(
        [upper.reshape(STEPS, CHUNK, HALF_X), lower.reshape(STEPS, CHUNK, HALF_X)], axis=1
    )
    whole = pieces.reshape(NX, HALF_X).astype(np.float32)
    high = whole.astype(ml_dtypes.bfloat16)
    low = (whole - high.astype(np.float32)).astype(ml_dtypes.bfloat16)
    return np.stack([high, low])


def horner(variable, coefficients):
    total = jnp.full_like(variable, coefficients[-1])
    for coefficient in coefficients[-2::-1]:
        total = total * variable + coefficient
    return total


SINE = [(-1.0) ** k / math.factorial(2 * k + 1) for k in range(8)]
COSINE = [(-1.0) ** k / math.factorial(2 * k) for k in range(8)]


def small_sincos(angle):
    square = angle * angle
    return angle * horner(square, SINE), horner(square, COSINE)


def cycles_sincos(cycles):
    cycles = cycles - jnp.round(cycles)
    sine, cosine = small_sincos(cycles * math.pi)
    return 2.0 * sine * cosine, 1.0 - 2.0 * sine * sine


def own_place():
    z_at, x_high, y_at, core = (lax.axis_index(name) for name in ROW_AXES)
    return ((z_at * GRID_XH + x_high) * GRID_Y + y_at) * GRID_CORE + core, core


def local_kernel(
    facts_ref,
    table_hbm,
    intens_hbm,
    keep_ref,
    send_ref,
    values,
    table_ref,
    shift_base,
    shift_ref,
    coarse_ref,
    fine_ref,
    middle_ref,
    masks_ref,
    middle_used,
    rotated,
    products,
    copy_sem,
):
    own_row, own_core = own_place()
    table_copies = []
    for step in range(STEPS):
        rows = pl.ds(step * 2 * CHUNK, 2 * CHUNK)
        table_copies.append(
            pltpu.make_async_copy(table_hbm.at[rows], table_ref.at[rows], copy_sem.at[step])
        )
    block_copies = []
    for block in range(BLK_BAND):
        block_copies.append([])
        for row in range(ROWS_DEV):
            block_copies[block].append(
                pltpu.make_async_copy(
                    intens_hbm.at[row, :, pl.ds(block * PIX_BLK, PIX_BLK)],
                    values.at[:, pl.ds(block * GROUP + row * PIX_BLK, PIX_BLK)],
                    copy_sem.at[STEPS + block * ROWS_DEV + row],
                )
            )
    for copy in table_copies[:1] + sum(block_copies, []) + table_copies[1:]:
        copy.start()

    gradient_x = facts_ref[1:2, 0:PIX_BAND]
    gradient_y = facts_ref[2:3, 0:PIX_BAND]
    eights = lax.broadcasted_iota(jnp.int32, (HALF_X // 8, PIX_BAND), 0).astype(F32)
    coarse_ref[0], coarse_ref[1] = cycles_sincos(gradient_x * (eights * (8.0 / NX)))
    units = lax.broadcasted_iota(jnp.int32, (8, PIX_BAND), 0).astype(F32)
    fine_ref[0], fine_ref[1] = cycles_sincos(gradient_x * (units * (1.0 / NX)))
    middle_ref[0:1, :], middle_ref[1:2, :] = cycles_sincos(gradient_x * 0.5)

    def make_masks():
        block_ids = lax.broadcasted_iota(jnp.int32, (8, NX), 0)
        packed = facts_ref[0:1, :].astype(jnp.int32)
        counts = packed >> 4
        used = (((packed & 3) == block_ids) & (counts > 0)) | (
            (((packed >> 2) & 3) == block_ids) & (counts > 1)
        )
        used = used.astype(F32)
        place_sum = lax.broadcasted_iota(
            jnp.int32, (HALF_X, HALF_X), 0
        ) + lax.broadcasted_iota(jnp.int32, (HALF_X, HALF_X), 1)
        reverse = (place_sum == HALF_X).astype(F32).astype(BF16)
        mirror = jnp.dot(
            used[:, HALF_X:].astype(BF16), reverse, preferred_element_type=F32
        )
        lane_first = lax.broadcasted_iota(jnp.int32, (8, HALF_X), 1) == 0
        ahead = used[:, :HALF_X]
        mirror = jnp.where(lane_first, ahead, mirror)
        for sort, rows in enumerate((ahead + mirror, ahead - mirror)):
            columns = rows.T
            for block in range(BLK_BAND):
                masks_ref[sort * BLK_BAND + block] = jnp.broadcast_to(
                    columns[:, block : block + 1], (HALF_X, PIX_BLK)
                ).astype(BF16)
        middle_used[...] = jnp.broadcast_to(used[:, HALF_X : HALF_X + 1], (8, PIX_BLK))

    upper_rows = lax.broadcasted_iota(jnp.int32, (8, PIX_BLK), 0) < ROWS_DEV

    def shift_block(block):
        lanes = slice(block * PIX_BLK, (block + 1) * PIX_BLK)
        gradient = gradient_y[:, lanes]
        nearest = jnp.round(gradient)
        rest = gradient - nearest
        sinc = horner(rest * rest, [SINE[k] * math.pi ** (2 * k) for k in range(8)])
        small = rest * (math.pi / NY)
        peak = sinc * (1.0 - small * small * (1.0 / 3.0))
        parity = nearest - 2.0 * jnp.floor(nearest * 0.5)
        lobes = (1.0 - 2.0 * parity) * (rest * math.pi) * sinc * (1.0 / NY)
        sine_g, cosine_g = small_sincos(gradient * (math.pi / NY))
        first_row = lax.broadcasted_iota(jnp.int32, (TALL - NY, PIX_BLK), 0) == 0
        for row in range(ROWS_DEV):
            column = block * GROUP + row * PIX_BLK
            shift_ref[NY:TALL, column : column + PIX_BLK] = jnp.where(
                first_row, lobes * (1.0 - 2.0 * (row % 2)), 0.0
            ).astype(BF16)
        for half in range(GRID_CORE):
            core = own_core if half == 0 else 1 - own_core
            offset = (
                lax.broadcasted_iota(jnp.int32, (NY, PIX_BLK), 0)
                - (ROWS_DEV - 1)
                + ROWS_DEV * (core - own_row)
            )
            distance = offset.astype(F32)
            folded = distance - NY * jnp.round(distance * (1.0 / NY))
            sine_d, cosine_d = small_sincos(folded * (math.pi / NY))
            row_sign = (1 - 2 * (offset & 1)).astype(F32)
            upper = (cosine_d * cosine_g + sine_d * sine_g) * row_sign
            lower = sine_d * cosine_g - cosine_d * sine_g
            turns = (distance - nearest) * (1.0 / NY)
            at_peak = turns == jnp.round(turns)
            lower = jnp.where(at_peak, 1.0, lower)
            shift_base[...] = jnp.where(at_peak, peak, -lobes * upper / lower)
            for place in range(GRID_XH * GRID_Y):
                for quad in range(GRID_Z // 4):
                    tiles = []
                    for pair in range(2):
                        start = (quad * 4 + pair * 2) * 64 + place * 8
                        tiles.append(
                            (shift_base[start : start + 8, :], shift_base[start + 64 : start + 72, :])
                        )
                    target = half * (NY // 2) + place * 32 + quad * 16
                    for row in range(ROWS_DEV):
                        column = block * GROUP + row * PIX_BLK
                        merged = []
                        for left, right in tiles:
                            if row < ROWS_DEV - 1:
                                left = pltpu.roll(left, 5 + row, 0)
                            merged.append(
                                jnp.where(upper_rows, left, pltpu.roll(right, 1 + row, 0))
                            )
                        shift_ref[target : target + 16, column : column + PIX_BLK] = (
                            jnp.concatenate(merged, axis=0).astype(BF16)
                        )

    def transform(step, block):
        return jnp.dot(
            table_ref[step * 2 * CHUNK : (step + 1) * 2 * CHUNK, :],
            values[:, block * GROUP : (block + 1) * GROUP],
            preferred_element_type=F32,
        )

    def rotate(step, block, spectrum):
        lanes = slice(block * PIX_BLK, (block + 1) * PIX_BLK)
        spectrum = spectrum.astype(BF16).astype(F32)
        fine_sine, fine_cosine = fine_ref[0, :, lanes], fine_ref[1, :, lanes]
        sines, cosines = [], []
        for octet in range(step * CHUNK // 8, (step + 1) * CHUNK // 8):
            sine_c = coarse_ref[0, octet : octet + 1, lanes]
            cosine_c = coarse_ref[1, octet : octet + 1, lanes]
            sines.append(sine_c * fine_cosine + cosine_c * fine_sine)
            cosines.append(cosine_c * fine_cosine - sine_c * fine_sine)
        sine_p = jnp.concatenate(sines, axis=0)
        cosine_p = jnp.concatenate(cosines, axis=0)
        plus = masks_ref[block, step * CHUNK : (step + 1) * CHUNK]
        minus = masks_ref[BLK_BAND + block, step * CHUNK : (step + 1) * CHUNK]
        for row in range(ROWS_DEV):
            inner = slice(row * PIX_BLK, (row + 1) * PIX_BLK)
            outer = slice(block * GROUP + row * PIX_BLK, block * GROUP + (row + 1) * PIX_BLK)
            real_part = spectrum[:CHUNK, inner]
            imag_part = spectrum[CHUNK:, inner]
            turned_real = (real_part * cosine_p + imag_part * sine_p).astype(BF16)
            turned_imag = (imag_part * cosine_p - real_part * sine_p).astype(BF16)
            rotated[step, 0:CHUNK, outer] = turned_real * plus
            rotated[step, CHUNK : 2 * CHUNK, outer] = turned_imag * plus
            rotated[step, 2 * CHUNK : 3 * CHUNK, outer] = turned_imag * minus
            rotated[step, 3 * CHUNK :, outer] = -turned_real * minus
            if step == 0:
                only = imag_part[0:1] * middle_used[block : block + 1, :]
                top = lax.broadcasted_iota(jnp.int32, (16, PIX_BLK), 0) == 0
                for start, which in ((CHUNK, 1), (3 * CHUNK, 0)):
                    old = rotated[step, start : start + 16, outer].astype(F32)
                    rotated[step, start : start + 16, outer] = jnp.where(
                        top, only * middle_ref[which : which + 1, lanes], old
                    ).astype(BF16)

    def multiply(step):
        products[step] = lax.dot_general(
            shift_ref[...],
            rotated[step],
            (((1,), (1,)), ((), ())),
            preferred_element_type=F32,
        )

    even = (lax.broadcasted_iota(jnp.int32, (32, 2 * CHUNK), 0) & 1) == 0

    def store(step):
        edge_herm = products[step, NY : NY + 1, : 2 * CHUNK]
        edge_anti = products[step, NY : NY + 1, 2 * CHUNK :]
        edges = (
            jnp.where(even, -edge_anti, edge_anti),
            jnp.where(even, edge_herm, -edge_herm),
        )
        for half, out_ref in enumerate((keep_ref, send_ref)):
            for place in range(GRID_XH * GRID_Y):
                start = half * (NY // 2) + place * 32
                for band in range(GRID_BAND):
                    slots = slice(band * 2 * CHUNK, (band + 1) * 2 * CHUNK)
                    whole = (products[step, start : start + 32, slots] + edges[band]).astype(
                        out_ref.dtype
                    )
                    for tile in range(2 * CHUNK // PIX_BLK):
                        target = (step * (2 * CHUNK // PIX_BLK) + tile) * 32
                        out_ref[place * GRID_BAND + band, target : target + 32, :] = whole[
                            :, tile * PIX_BLK : (tile + 1) * PIX_BLK
                        ]

    def wait_for(copies):
        for copy in copies:
            copy.wait()

    make_masks()
    for block in range(BLK_BAND):
        shift_block(block)
    wait_for(table_copies[:1] + block_copies[0])
    rotate(0, 0, transform(0, 0))
    wait_for(block_copies[1])
    rotate(0, 1, transform(0, 1))
    wait_for(block_copies[2] + table_copies[1:])
    rotate(0, 2, transform(0, 2))
    multiply(0)
    rotate(1, 0, transform(1, 0))
    rotate(1, 1, transform(1, 1))
    store(0)
    rotate(1, 2, transform(1, 2))
    multiply(1)
    store(1)


VMEM_SPEC = pl.BlockSpec(memory_space=pltpu.VMEM)
HBM_SPEC = pl.BlockSpec(memory_space=pltpu.HBM)
LOCAL_VMEM = 50 * 1024 * 1024


def local_part(facts, table, intens):
    shape = (PIECES, 32 * GRID_Z, PIX_BLK)
    return pl.pallas_call(
        local_kernel,
        in_specs=[VMEM_SPEC, HBM_SPEC, HBM_SPEC],
        out_specs=[VMEM_SPEC] * 2,
        out_shape=[jax.ShapeDtypeStruct(shape, F32), jax.ShapeDtypeStruct(shape, BF16)],
        scratch_shapes=[
            pltpu.VMEM((NX, DEPTH), BF16),
            pltpu.VMEM((NX, NX), BF16),
            pltpu.VMEM((NY, PIX_BLK), F32),
            pltpu.VMEM((TALL, DEPTH), BF16),
            pltpu.VMEM((2, HALF_X // 8, PIX_BAND), F32),
            pltpu.VMEM((2, 8, PIX_BAND), F32),
            pltpu.VMEM((2, PIX_BAND), F32),
            pltpu.VMEM((2 * BLK_BAND, HALF_X, PIX_BLK), BF16),
            pltpu.VMEM((8, PIX_BLK), F32),
            pltpu.VMEM((STEPS, 4 * CHUNK, DEPTH), BF16),
            pltpu.VMEM((STEPS, TALL, 4 * CHUNK), F32),
            pltpu.SemaphoreType.DMA((STEPS + BLK_BAND * ROWS_DEV,)),
        ],
        compiler_params=pltpu.CompilerParams(vmem_limit_bytes=LOCAL_VMEM),
    )(facts, table, intens)


def plane_kernel(pieces_ref, plane_ref):
    total = pieces_ref[0].astype(F32)
    for source in range(1, PIECES):
        total = total + pieces_ref[source].astype(F32)
    for z_at in range(GRID_Z):
        rows = [
            total[tile * 32 + z_at * ROWS_DEV : tile * 32 + (z_at + 1) * ROWS_DEV]
            for tile in range(NX // PIX_BLK)
        ]
        plane_ref[z_at] = jnp.concatenate(rows, axis=0).astype(BF16)


def plane_part(pieces):
    return pl.pallas_call(
        plane_kernel,
        in_specs=[VMEM_SPEC],
        out_specs=VMEM_SPEC,
        out_shape=jax.ShapeDtypeStruct((GRID_Z, 32, PIX_BLK), BF16),
        compiler_params=pltpu.CompilerParams(vmem_limit_bytes=32 * 1024 * 1024),
    )(pieces)


def final_kernel(parts_ref, table_ref, image_ref):
    total = parts_ref[0].astype(F32)
    for source in range(1, GRID_Z):
        total = total + parts_ref[source].astype(F32)
    tiles = [total[at : at + ROWS_DEV] for at in range(0, 32, ROWS_DEV)]
    total = jnp.concatenate(tiles, axis=1)
    high = total.astype(BF16).astype(F32)
    low = total - high
    odd_slot = (lax.broadcasted_iota(jnp.int32, (ROWS_DEV, NX), 1) & 1) == 1
    high_even, high_odd = jnp.where(odd_slot, 0.0, high), jnp.where(odd_slot, high, 0.0)
    low_even, low_odd = jnp.where(odd_slot, 0.0, low), jnp.where(odd_slot, low, 0.0)
    rows = jnp.concatenate([high_even, high_odd, low_even, low_odd], axis=0).astype(BF16)
    image = jnp.dot(rows, table_ref[0], preferred_element_type=F32)
    image = image[: 2 * ROWS_DEV] + image[2 * ROWS_DEV :]
    image = image + jnp.dot(
        rows[: 2 * ROWS_DEV], table_ref[1], preferred_element_type=F32
    )
    even, odd = image[:ROWS_DEV], image[ROWS_DEV:]
    image_ref[0, :, :HALF_X] = even + odd
    image_ref[0, :, HALF_X:] = even - odd


def final_part(parts, table):
    return pl.pallas_call(
        final_kernel,
        in_specs=[VMEM_SPEC] * 2,
        out_specs=VMEM_SPEC,
        out_shape=jax.ShapeDtypeStruct((1, ROWS_DEV, NX), F32),
        compiler_params=pltpu.CompilerParams(vmem_limit_bytes=32 * 1024 * 1024),
    )(parts, table)


def body(intens, block_list, block_count, pixel_gradient):
    packed = block_list[:, 0] + 4 * block_list[:, 1] + 16 * block_count[:, 0]
    facts = jnp.concatenate(
        [
            packed.astype(F32)[None],
            jnp.pad(pixel_gradient, ((0, 5), (0, NX - PIX_BAND))),
        ],
        axis=0,
    )
    keep, send = local_part(facts, jnp.asarray(forward_table()), intens)
    received = lax.ppermute(send, "core", [(0, 1), (1, 0)])
    chip = (keep + received.astype(F32)).astype(BF16)
    pieces = lax.all_to_all(
        chip, ("xh", "y", "band"), split_axis=0, concat_axis=0, tiled=True
    )
    plane = plane_part(pieces)
    parts = lax.all_to_all(plane, "z", split_axis=0, concat_axis=0, tiled=True)
    return final_part(parts, jnp.asarray(backward_table()))


def solution(mesh):
    grid = Mesh(
        mesh.devices.reshape(GRID_Z, GRID_XH, GRID_Y, GRID_CORE, GRID_BAND),
        ROW_AXES + ("band",),
    )
    return jax.shard_map(
        body,
        mesh=grid,
        in_specs=(P(ROW_AXES, None, "band"), P(None, "band"), P(None, "band"), P(None, "band")),
        out_specs=P("band", ROW_AXES, None),
        check_vma=False,
    )
```

```python
import math

import jax
import jax.numpy as jnp
import ml_dtypes
import numpy as np
from jax import lax
from jax.experimental import pallas as pl
from jax.experimental.pallas import tpu as pltpu
from jax.sharding import Mesh
from jax.sharding import PartitionSpec as P

NX = 1024
NY = 512
PIX_BLK = 128
BLK_BAND = 3
PIX_BAND = PIX_BLK * BLK_BAND
ROWS_DEV = 4
CAP = 2
HALF_X = NX // 2
CHUNK = 256
STEPS = HALF_X // CHUNK
GROUP = ROWS_DEV * PIX_BLK
DEPTH = BLK_BAND * GROUP
TALL = NY + 16
GRID_Z, GRID_XH, GRID_Y, GRID_CORE, GRID_BAND = 8, 2, 4, 2, 2
PIECES = GRID_XH * GRID_Y * GRID_BAND
ROW_AXES = ("z", "xh", "y", "core")
F32, BF16 = jnp.float32, jnp.bfloat16


def forward_table():
    turns = np.outer(np.arange(HALF_X + 1), np.arange(NX)) % NX
    angle = turns.astype(np.float32) * np.float32(2.0 * math.pi / NX)
    norm_factor = np.float32(1.0 / math.sqrt(NX))
    cosine, sine = np.cos(angle) * norm_factor, np.sin(angle) * norm_factor
    lower = -sine[:HALF_X]
    lower[0] = cosine[HALF_X]
    pieces = np.stack(
        [cosine[:HALF_X].reshape(STEPS, CHUNK, NX), lower.reshape(STEPS, CHUNK, NX)], axis=1
    )
    return pieces.reshape(NX, NX).astype(ml_dtypes.bfloat16)


def backward_table():
    turns = np.outer(np.arange(HALF_X + 1), np.arange(HALF_X)) % NX
    angle = turns.astype(np.float64) * (2.0 * math.pi / NX)
    scale = 1.0 / math.sqrt(NX) / math.sqrt(GRID_BAND * CAP * PIX_BLK)
    upper = np.cos(angle[:HALF_X]) * scale
    upper[0] *= 0.5
    lower = -np.sin(angle[:HALF_X]) * scale
    lower[0] = np.cos(angle[HALF_X]) * scale
    pieces = np.stack(
        [upper.reshape(STEPS, CHUNK, HALF_X), lower.reshape(STEPS, CHUNK, HALF_X)], axis=1
    )
    whole = pieces.reshape(NX, HALF_X).astype(np.float32)
    high = whole.astype(ml_dtypes.bfloat16)
    low = (whole - high.astype(np.float32)).astype(ml_dtypes.bfloat16)
    return np.stack([high, low])


def horner(variable, coefficients):
    total = jnp.full_like(variable, coefficients[-1])
    for coefficient in coefficients[-2::-1]:
        total = total * variable + coefficient
    return total


SINE = [(-1.0) ** k / math.factorial(2 * k + 1) for k in range(8)]
COSINE = [(-1.0) ** k / math.factorial(2 * k) for k in range(8)]


def small_sincos(angle):
    square = angle * angle
    return angle * horner(square, SINE), horner(square, COSINE)


def cycles_sincos(cycles):
    cycles = cycles - jnp.round(cycles)
    sine, cosine = small_sincos(cycles * math.pi)
    return 2.0 * sine * cosine, 1.0 - 2.0 * sine * sine


def own_place():
    z_at, x_high, y_at, core = (lax.axis_index(name) for name in ROW_AXES)
    return ((z_at * GRID_XH + x_high) * GRID_Y + y_at) * GRID_CORE + core, core


def local_kernel(
    facts_ref,
    table_hbm,
    intens_hbm,
    keep_ref,
    send_ref,
    values,
    table_ref,
    shift_base,
    shift_ref,
    coarse_ref,
    fine_ref,
    middle_ref,
    masks_ref,
    middle_used,
    rotated,
    products,
    copy_sem,
):
    own_row, own_core = own_place()
    table_copies = []
    for step in range(STEPS):
        rows = pl.ds(step * 2 * CHUNK, 2 * CHUNK)
        table_copies.append(
            pltpu.make_async_copy(table_hbm.at[rows], table_ref.at[rows], copy_sem.at[step])
        )
    block_copies = []
    for block in range(BLK_BAND):
        block_copies.append([])
        for row in range(ROWS_DEV):
            block_copies[block].append(
                pltpu.make_async_copy(
                    intens_hbm.at[row, :, pl.ds(block * PIX_BLK, PIX_BLK)],
                    values.at[:, pl.ds(block * GROUP + row * PIX_BLK, PIX_BLK)],
                    copy_sem.at[STEPS + block * ROWS_DEV + row],
                )
            )
    for copy in table_copies[:1] + block_copies[0]:
        copy.start()

    gradient_x = facts_ref[1:2, 0:PIX_BAND]
    gradient_y = facts_ref[2:3, 0:PIX_BAND]
    eights = lax.broadcasted_iota(jnp.int32, (HALF_X // 8, PIX_BAND), 0).astype(F32)
    coarse_ref[0], coarse_ref[1] = cycles_sincos(gradient_x * (eights * (8.0 / NX)))
    units = lax.broadcasted_iota(jnp.int32, (8, PIX_BAND), 0).astype(F32)
    fine_ref[0], fine_ref[1] = cycles_sincos(gradient_x * (units * (1.0 / NX)))
    middle_ref[0:1, :], middle_ref[1:2, :] = cycles_sincos(gradient_x * 0.5)

    def make_masks():
        block_ids = lax.broadcasted_iota(jnp.int32, (8, NX), 0)
        packed = facts_ref[0:1, :].astype(jnp.int32)
        counts = packed >> 4
        used = (((packed & 3) == block_ids) & (counts > 0)) | (
            (((packed >> 2) & 3) == block_ids) & (counts > 1)
        )
        used = used.astype(F32)
        place_sum = lax.broadcasted_iota(
            jnp.int32, (HALF_X, HALF_X), 0
        ) + lax.broadcasted_iota(jnp.int32, (HALF_X, HALF_X), 1)
        reverse = (place_sum == HALF_X).astype(F32).astype(BF16)
        mirror = jnp.dot(
            used[:, HALF_X:].astype(BF16), reverse, preferred_element_type=F32
        )
        lane_first = lax.broadcasted_iota(jnp.int32, (8, HALF_X), 1) == 0
        ahead = used[:, :HALF_X]
        mirror = jnp.where(lane_first, ahead, mirror)
        for sort, rows in enumerate((ahead + mirror, ahead - mirror)):
            columns = rows.T
            for block in range(BLK_BAND):
                masks_ref[sort * BLK_BAND + block] = jnp.broadcast_to(
                    columns[:, block : block + 1], (HALF_X, PIX_BLK)
                ).astype(BF16)
        middle_used[...] = jnp.broadcast_to(used[:, HALF_X : HALF_X + 1], (8, PIX_BLK))

    upper_rows = lax.broadcasted_iota(jnp.int32, (8, PIX_BLK), 0) < ROWS_DEV

    def shift_block(block):
        lanes = slice(block * PIX_BLK, (block + 1) * PIX_BLK)
        gradient = gradient_y[:, lanes]
        nearest = jnp.round(gradient)
        rest = gradient - nearest
        sinc = horner(rest * rest, [SINE[k] * math.pi ** (2 * k) for k in range(8)])
        small = rest * (math.pi / NY)
        peak = sinc * (1.0 - small * small * (1.0 / 3.0))
        parity = nearest - 2.0 * jnp.floor(nearest * 0.5)
        lobes = (1.0 - 2.0 * parity) * (rest * math.pi) * sinc * (1.0 / NY)
        sine_g, cosine_g = small_sincos(gradient * (math.pi / NY))
        first_row = lax.broadcasted_iota(jnp.int32, (TALL - NY, PIX_BLK), 0) == 0
        for row in range(ROWS_DEV):
            column = block * GROUP + row * PIX_BLK
            shift_ref[NY:TALL, column : column + PIX_BLK] = jnp.where(
                first_row, lobes * (1.0 - 2.0 * (row % 2)), 0.0
            ).astype(BF16)
        for half in range(GRID_CORE):
            core = own_core if half == 0 else 1 - own_core
            offset = (
                lax.broadcasted_iota(jnp.int32, (NY, PIX_BLK), 0)
                - (ROWS_DEV - 1)
                + ROWS_DEV * (core - own_row)
            )
            distance = offset.astype(F32)
            folded = distance - NY * jnp.round(distance * (1.0 / NY))
            sine_d, cosine_d = small_sincos(folded * (math.pi / NY))
            row_sign = (1 - 2 * (offset & 1)).astype(F32)
            upper = (cosine_d * cosine_g + sine_d * sine_g) * row_sign
            lower = sine_d * cosine_g - cosine_d * sine_g
            turns = (distance - nearest) * (1.0 / NY)
            at_peak = turns == jnp.round(turns)
            lower = jnp.where(at_peak, 1.0, lower)
            shift_base[...] = jnp.where(at_peak, peak, -lobes * upper / lower)
            for place in range(GRID_XH * GRID_Y):
                for quad in range(GRID_Z // 4):
                    tiles = []
                    for pair in range(2):
                        start = (quad * 4 + pair * 2) * 64 + place * 8
                        tiles.append(
                            (shift_base[start : start + 8, :], shift_base[start + 64 : start + 72, :])
                        )
                    target = half * (NY // 2) + place * 32 + quad * 16
                    for row in range(ROWS_DEV):
                        column = block * GROUP + row * PIX_BLK
                        merged = []
                        for left, right in tiles:
                            if row < ROWS_DEV - 1:
                                left = pltpu.roll(left, 5 + row, 0)
                            merged.append(
                                jnp.where(upper_rows, left, pltpu.roll(right, 1 + row, 0))
                            )
                        shift_ref[target : target + 16, column : column + PIX_BLK] = (
                            jnp.concatenate(merged, axis=0).astype(BF16)
                        )

    def transform(step, block):
        return jnp.dot(
            table_ref[step * 2 * CHUNK : (step + 1) * 2 * CHUNK, :],
            values[:, block * GROUP : (block + 1) * GROUP],
            preferred_element_type=F32,
        )

    def rotate(step, block, spectrum):
        lanes = slice(block * PIX_BLK, (block + 1) * PIX_BLK)
        spectrum = spectrum.astype(BF16).astype(F32)
        fine_sine, fine_cosine = fine_ref[0, :, lanes], fine_ref[1, :, lanes]
        sines, cosines = [], []
        for octet in range(step * CHUNK // 8, (step + 1) * CHUNK // 8):
            sine_c = coarse_ref[0, octet : octet + 1, lanes]
            cosine_c = coarse_ref[1, octet : octet + 1, lanes]
            sines.append(sine_c * fine_cosine + cosine_c * fine_sine)
            cosines.append(cosine_c * fine_cosine - sine_c * fine_sine)
        sine_p = jnp.concatenate(sines, axis=0)
        cosine_p = jnp.concatenate(cosines, axis=0)
        plus = masks_ref[block, step * CHUNK : (step + 1) * CHUNK]
        minus = masks_ref[BLK_BAND + block, step * CHUNK : (step + 1) * CHUNK]
        for row in range(ROWS_DEV):
            inner = slice(row * PIX_BLK, (row + 1) * PIX_BLK)
            outer = slice(block * GROUP + row * PIX_BLK, block * GROUP + (row + 1) * PIX_BLK)
            real_part = spectrum[:CHUNK, inner]
            imag_part = spectrum[CHUNK:, inner]
            turned_real = (real_part * cosine_p + imag_part * sine_p).astype(BF16)
            turned_imag = (imag_part * cosine_p - real_part * sine_p).astype(BF16)
            rotated[step, 0:CHUNK, outer] = turned_real * plus
            rotated[step, CHUNK : 2 * CHUNK, outer] = turned_imag * plus
            rotated[step, 2 * CHUNK : 3 * CHUNK, outer] = turned_imag * minus
            rotated[step, 3 * CHUNK :, outer] = -turned_real * minus
            if step == 0:
                only = imag_part[0:1] * middle_used[block : block + 1, :]
                top = lax.broadcasted_iota(jnp.int32, (16, PIX_BLK), 0) == 0
                for start, which in ((CHUNK, 1), (3 * CHUNK, 0)):
                    old = rotated[step, start : start + 16, outer].astype(F32)
                    rotated[step, start : start + 16, outer] = jnp.where(
                        top, only * middle_ref[which : which + 1, lanes], old
                    ).astype(BF16)

    def multiply(step):
        products[step] = lax.dot_general(
            shift_ref[...],
            rotated[step],
            (((1,), (1,)), ((), ())),
            preferred_element_type=F32,
        )

    even = (lax.broadcasted_iota(jnp.int32, (32, 2 * CHUNK), 0) & 1) == 0

    def store(step):
        edge_herm = products[step, NY : NY + 1, : 2 * CHUNK]
        edge_anti = products[step, NY : NY + 1, 2 * CHUNK :]
        edges = (
            jnp.where(even, -edge_anti, edge_anti),
            jnp.where(even, edge_herm, -edge_herm),
        )
        for half, out_ref in enumerate((keep_ref, send_ref)):
            for place in range(GRID_XH * GRID_Y):
                start = half * (NY // 2) + place * 32
                for band in range(GRID_BAND):
                    slots = slice(band * 2 * CHUNK, (band + 1) * 2 * CHUNK)
                    whole = (products[step, start : start + 32, slots] + edges[band]).astype(
                        out_ref.dtype
                    )
                    for tile in range(2 * CHUNK // PIX_BLK):
                        target = (step * (2 * CHUNK // PIX_BLK) + tile) * 32
                        out_ref[place * GRID_BAND + band, target : target + 32, :] = whole[
                            :, tile * PIX_BLK : (tile + 1) * PIX_BLK
                        ]

    def wait_for(copies):
        for copy in copies:
            copy.wait()

    for copy in block_copies[1] + block_copies[2] + table_copies[1:]:
        copy.start()
    make_masks()
    shift_block(0)
    shift_block(1)
    wait_for(table_copies[:1] + block_copies[0])
    rotate(0, 0, transform(0, 0))
    wait_for(block_copies[1])
    rotate(0, 1, transform(0, 1))
    wait_for(block_copies[2] + table_copies[1:])
    rotate(0, 2, transform(0, 2))
    shift_block(2)
    multiply(0)
    rotate(1, 0, transform(1, 0))
    rotate(1, 1, transform(1, 1))
    store(0)
    rotate(1, 2, transform(1, 2))
    multiply(1)
    store(1)


VMEM_SPEC = pl.BlockSpec(memory_space=pltpu.VMEM)
HBM_SPEC = pl.BlockSpec(memory_space=pltpu.HBM)
LOCAL_VMEM = 50 * 1024 * 1024


def local_part(facts, table, intens):
    shape = (PIECES, 32 * GRID_Z, PIX_BLK)
    return pl.pallas_call(
        local_kernel,
        in_specs=[VMEM_SPEC, HBM_SPEC, HBM_SPEC],
        out_specs=[VMEM_SPEC] * 2,
        out_shape=[jax.ShapeDtypeStruct(shape, F32), jax.ShapeDtypeStruct(shape, BF16)],
        scratch_shapes=[
            pltpu.VMEM((NX, DEPTH), BF16),
            pltpu.VMEM((NX, NX), BF16),
            pltpu.VMEM((NY, PIX_BLK), F32),
            pltpu.VMEM((TALL, DEPTH), BF16),
            pltpu.VMEM((2, HALF_X // 8, PIX_BAND), F32),
            pltpu.VMEM((2, 8, PIX_BAND), F32),
            pltpu.VMEM((2, PIX_BAND), F32),
            pltpu.VMEM((2 * BLK_BAND, HALF_X, PIX_BLK), BF16),
            pltpu.VMEM((8, PIX_BLK), F32),
            pltpu.VMEM((STEPS, 4 * CHUNK, DEPTH), BF16),
            pltpu.VMEM((STEPS, TALL, 4 * CHUNK), F32),
            pltpu.SemaphoreType.DMA((STEPS + BLK_BAND * ROWS_DEV,)),
        ],
        compiler_params=pltpu.CompilerParams(vmem_limit_bytes=LOCAL_VMEM),
    )(facts, table, intens)


def plane_kernel(pieces_ref, plane_ref):
    total = pieces_ref[0].astype(F32)
    for source in range(1, PIECES):
        total = total + pieces_ref[source].astype(F32)
    for z_at in range(GRID_Z):
        rows = [
            total[tile * 32 + z_at * ROWS_DEV : tile * 32 + (z_at + 1) * ROWS_DEV]
            for tile in range(NX // PIX_BLK)
        ]
        plane_ref[z_at] = jnp.concatenate(rows, axis=0).astype(BF16)


def plane_part(pieces):
    return pl.pallas_call(
        plane_kernel,
        in_specs=[VMEM_SPEC],
        out_specs=VMEM_SPEC,
        out_shape=jax.ShapeDtypeStruct((GRID_Z, 32, PIX_BLK), BF16),
        compiler_params=pltpu.CompilerParams(vmem_limit_bytes=32 * 1024 * 1024),
    )(pieces)


def final_kernel(parts_ref, table_ref, image_ref):
    total = parts_ref[0].astype(F32)
    for source in range(1, GRID_Z):
        total = total + parts_ref[source].astype(F32)
    tiles = [total[at : at + ROWS_DEV] for at in range(0, 32, ROWS_DEV)]
    total = jnp.concatenate(tiles, axis=1)
    high = total.astype(BF16).astype(F32)
    low = total - high
    odd_slot = (lax.broadcasted_iota(jnp.int32, (ROWS_DEV, NX), 1) & 1) == 1
    high_even, high_odd = jnp.where(odd_slot, 0.0, high), jnp.where(odd_slot, high, 0.0)
    low_even, low_odd = jnp.where(odd_slot, 0.0, low), jnp.where(odd_slot, low, 0.0)
    rows = jnp.concatenate([high_even, high_odd, low_even, low_odd], axis=0).astype(BF16)
    image = jnp.dot(rows, table_ref[0], preferred_element_type=F32)
    image = image[: 2 * ROWS_DEV] + image[2 * ROWS_DEV :]
    image = image + jnp.dot(
        rows[: 2 * ROWS_DEV], table_ref[1], preferred_element_type=F32
    )
    even, odd = image[:ROWS_DEV], image[ROWS_DEV:]
    image_ref[0, :, :HALF_X] = even + odd
    image_ref[0, :, HALF_X:] = even - odd


def final_part(parts, table):
    return pl.pallas_call(
        final_kernel,
        in_specs=[VMEM_SPEC] * 2,
        out_specs=VMEM_SPEC,
        out_shape=jax.ShapeDtypeStruct((1, ROWS_DEV, NX), F32),
        compiler_params=pltpu.CompilerParams(vmem_limit_bytes=32 * 1024 * 1024),
    )(parts, table)


def body(intens, block_list, block_count, pixel_gradient):
    packed = block_list[:, 0] + 4 * block_list[:, 1] + 16 * block_count[:, 0]
    facts = jnp.concatenate(
        [
            packed.astype(F32)[None],
            jnp.pad(pixel_gradient, ((0, 5), (0, NX - PIX_BAND))),
        ],
        axis=0,
    )
    keep, send = local_part(facts, jnp.asarray(forward_table()), intens)
    received = lax.ppermute(send, "core", [(0, 1), (1, 0)])
    chip = (keep + received.astype(F32)).astype(BF16)
    pieces = lax.all_to_all(
        chip, ("xh", "y", "band"), split_axis=0, concat_axis=0, tiled=True
    )
    plane = plane_part(pieces)
    parts = lax.all_to_all(plane, "z", split_axis=0, concat_axis=0, tiled=True)
    return final_part(parts, jnp.asarray(backward_table()))


def solution(mesh):
    grid = Mesh(
        mesh.devices.reshape(GRID_Z, GRID_XH, GRID_Y, GRID_CORE, GRID_BAND),
        ROW_AXES + ("band",),
    )
    return jax.shard_map(
        body,
        mesh=grid,
        in_specs=(P(ROW_AXES, None, "band"), P(None, "band"), P(None, "band"), P(None, "band")),
        out_specs=P("band", ROW_AXES, None),
        check_vma=False,
    )
```
